256 devices in a mesh: dp: 4 (over z_lo, core), row: 16 (over x, y), col: 4 (over z_hi).
Axes of the slice: x: 4, y: 4, z: 8 (z_hi: 4, z_lo: 2; z = z_hi * 2 + z_lo), core: 2. Of those that a mesh axis runs over, the one named last changes fastest.
Arguments:
- activations: bfloat16 [8192, 8192], P('dp', 'row'), may hold values from -24 to 24
- out_grads: bfloat16 [8192, 16384], P(('dp', 'row'), 'col'), may hold values from -24 to 24
- weights: float32 [16384, 8192], P(('col', 'dp'), 'row'), may hold values from -0.0625 to 0.0625
- momentum: bfloat16 [16384, 8192], P(('col', 'dp'), 'row'), may hold values from -3 to 3
- scores: float32 [16384, 8192], P(('col', 'dp'), 'row'), may hold values from -6 to 6
- row_moment: float32 [16384], P(('col', 'dp')), may hold values from 0.05 to 90
- col_moment: float32 [8192], P('row'), may hold values from 0.05 to 90
Outputs:
- weights_new: float32 [16384, 8192], P(('col', 'dp'), 'row')
- momentum_new: bfloat16 [16384, 8192], P(('col', 'dp'), 'row')
- scores_new: float32 [16384, 8192], P(('col', 'dp'), 'row')
- row_moment_new: float32 [16384], P(('col', 'dp'))
- col_moment_new: float32 [8192], P('row')
The draws below stay inside these ranges and needn't reach their ends.
All inputs are finite; a program needn't handle non-finite values.
Results may differ from the reference program's by a relative error of at most 0.004.
Values may be sent and summed in bfloat16 or wider, within the bound.
No kernel may reach another device: no remote copies, remote signals or barrier semaphores. Data moves between devices by JAX's collectives and lax.ppermute only.
A program may use at most 128 MiB of HBM per device.

```python
import math
import jax
import jax.numpy as jnp
from jax import lax

D = 8192
FF = 16384
TOKENS = 8192


def column_scale(key, length):
    rising = jnp.exp(math.log(3.0) * jnp.arange(length, dtype=jnp.float32) / length)
    spread = jnp.exp(jax.random.uniform(jax.random.fold_in(key, 21), (length,), jnp.float32, math.log(0.5), math.log(2.0)))
    return rising * spread


def moment_law(key, length):
    place = jnp.arange(length, dtype=jnp.int32)
    rising = jnp.exp(math.log(3.0) * place.astype(jnp.float32) / length)
    ladder = jnp.exp(math.log(0.1) + math.log(300.0) * jnp.arange(16, dtype=jnp.float32) / 15.0)
    order = jax.random.permutation(jax.random.fold_in(key, 31), 16)
    levels = ladder[order]
    block = place * 16 // length
    spread = jnp.exp(jax.random.uniform(jax.random.fold_in(key, 32), (length,), jnp.float32, math.log(0.5), 0.0))
    return levels[block] * rising * spread


def draw_activations(key, part):
    key = jax.random.fold_in(key, 1)
    scaling = column_scale(key, D)
    value_key = jax.random.fold_in(key, 5)
    values = jnp.clip(jax.random.normal(value_key, (TOKENS, D), jnp.float32), -4.0, 4.0)
    return (values * scaling[None, :]).astype(jnp.bfloat16)


def draw_out_grads(key, part):
    key = jax.random.fold_in(key, 2)
    scaling = column_scale(key, FF)
    value_key = jax.random.fold_in(key, 5)
    values = jnp.clip(jax.random.normal(value_key, (TOKENS, FF), jnp.float32), -4.0, 4.0)
    return (values * scaling[None, :]).astype(jnp.bfloat16)


def draw_row_moment(key, part):
    key = jax.random.fold_in(key, 3)
    return moment_law(key, FF)


def draw_col_moment(key, part):
    key = jax.random.fold_in(key, 4)
    return moment_law(key, D)


def level_of(rng, extent, split, least, high):
    def one(dim, shards_of):
        heights = jax.random.uniform(jax.random.fold_in(jax.random.fold_in(rng, 6), dim), (shards_of,), jnp.float32, least / len(split), high / len(split))
        return jnp.repeat(jnp.exp(heights), extent[dim] // shards_of).reshape((-1,) + (1,) * (len(extent) - dim - 1))

    factor_of = one(*split[0])
    for cut in split[1:]:
        factor_of = factor_of * one(*cut)
    return factor_of


def noise(own_key, shape, deviation, bound, cuts=(), kind=jnp.bfloat16):
    array = deviation * jax.random.normal(own_key, shape, jnp.float32)
    if cuts:
        array = array * level_of(own_key, shape, cuts, -0.22, 0.18)
    return jnp.clip(array, -bound, bound).astype(kind)


def setup_inputs(seed: int = 0) -> dict:
    key_of = jax.random.split(jax.random.key(seed), 8)
    activations = draw_activations(jax.random.fold_in(key_of[7], 71), 0)
    out_grads = draw_out_grads(jax.random.fold_in(key_of[7], 71), 0)
    weights = noise(key_of[2], (FF, D), D ** -0.5, 0.0625, ((0, 16), (1, 16)), jnp.float32)
    momentum = noise(key_of[3], (FF, D), 0.5, 3.0, ((0, 16), (1, 16)))
    scores = noise(key_of[4], (FF, D), 1.0, 6.0, ((0, 16), (1, 16)), jnp.float32)
    row_moment = draw_row_moment(jax.random.fold_in(key_of[7], 71), 0)
    col_moment = draw_col_moment(jax.random.fold_in(key_of[7], 71), 0)
    return dict(activations=activations, out_grads=out_grads, weights=weights, momentum=momentum, scores=scores, row_moment=row_moment, col_moment=col_moment)


def reference(activations, out_grads, weights, momentum, scores, row_moment, col_moment):
    act_wide = activations.astype(jnp.float32)
    grad_wide = out_grads.astype(jnp.float32)
    gradient = jnp.dot(grad_wide.T, act_wide, precision=lax.Precision.HIGHEST) * (1.0 / math.sqrt(TOKENS))
    squares = gradient * gradient + 1e-30
    row_moment_new = 0.8 * row_moment + 0.2 * lax.optimization_barrier(jnp.sum(squares, axis=1)) / D
    col_moment_new = 0.8 * col_moment + 0.2 * lax.optimization_barrier(jnp.sum(squares, axis=0)) / FF
    row_mean = jnp.sum(row_moment_new) / FF
    update = gradient * lax.rsqrt(row_moment_new[:, None] * col_moment_new[None, :] / row_mean)
    momentum_new = (0.9 * momentum.astype(jnp.float32) + 0.1 * update).astype(jnp.bfloat16)
    weights_new = weights - 0.01 * momentum_new.astype(jnp.float32)
    scores_new = scores - 50.0 * weights * gradient
    return (weights_new, momentum_new, scores_new, row_moment_new, col_moment_new)
```

```python
import math

import jax
import jax.numpy as jnp
from jax import lax
from jax.sharding import Mesh, PartitionSpec as P

D = 8192
FF = 16384
CHUNKS = 4
AXES = ("core", "x", "y")


def ring_pairs(phase, step):
    pairs = []
    for core in range(2):
        for x in range(4):
            for y in range(4):
                if core == phase:
                    to = (x + step) % 4 * 4 + y
                else:
                    to = x * 4 + (y + step) % 4
                pairs.append((core * 16 + x * 4 + y, core * 16 + to))
    return pairs


def shift(array, phase, step):
    return lax.ppermute(array, AXES, ring_pairs(phase, step))


def swap(array, axis):
    return lax.ppermute(array, axis, [(0, 1), (1, 0)])


def ring_gather(block, phase):
    half = block.shape[0] // 2
    below = shift(block, phase, 1)
    above = shift(block, phase, -1)
    far_low = shift(below[:half], phase, 1)
    far_high = shift(above[half:], phase, -1)
    return block, below, above, far_low, far_high


def product(grad_rows, act_rows):
    return lax.dot_general(
        grad_rows, act_rows, (((0,), (0,)), ((), ())), preferred_element_type=jnp.float32
    )


def total_over(vector, axes):
    spread = jnp.broadcast_to(vector[None], (16, vector.shape[0]))
    return jnp.sum(lax.all_to_all(spread, axes, 0, 0, tiled=True), axis=0)


def local(activations, out_grads, weights, momentum, scores, row_moment, col_moment):
    token_scale = 1.0 / math.sqrt(activations.shape[0] * 4)
    core, low = lax.axis_index("core"), lax.axis_index("zl")
    x, y = lax.axis_index("x"), lax.axis_index("y")
    first, second = jnp.where(core == 0, x, y), jnp.where(core == 0, y, x)

    acts = activations.reshape(4, 4, 128, 512)
    acts = jnp.where(core == 0, jnp.swapaxes(acts, 0, 1), acts)
    order = (0, -1, 1, 2)
    acts = jnp.concatenate(
        [lax.dynamic_index_in_dim(acts, (second + j) % 4, 0) for j in order], axis=0
    )
    acts = jnp.concatenate(
        [lax.dynamic_index_in_dim(acts, (first + i) % 4, 1) for i in order], axis=1
    ).reshape(4, 512, 512)

    rows = FF // 16
    part = rows // CHUNKS
    starts = [((low ^ a) * 2 + (core ^ b)) * rows for a in range(2) for b in range(2)]

    gradient = []
    for k in range(CHUNKS):
        block = jnp.concatenate(
            [lax.dynamic_slice_in_dim(out_grads, s + k * part, part, 1) for s in starts], axis=1
        )
        group = jnp.concatenate(ring_gather(block, 0), axis=0)
        own, below, above, far_low, far_high = ring_gather(group, 1)
        partial = product(own, acts[0])
        partial = partial + product(below, acts[1])
        partial = partial + product(above, acts[2])
        partial = partial + product(far_low, acts[3, :256]) + product(far_high, acts[3, 256:])
        partial = partial.reshape(2, 2, part, 512)
        chip = partial[:, 0] + swap(partial[:, 1].astype(jnp.bfloat16), "core").astype(jnp.float32)
        whole = chip[0] + swap(chip[1].astype(jnp.bfloat16), "zl").astype(jnp.float32)
        gradient.append(whole * token_scale)
    gradient = jnp.concatenate(gradient, axis=0)

    squares = gradient * gradient + 1e-30
    row_full = total_over(jnp.sum(squares, axis=1), ("x", "y"))
    row_moment_new = 0.8 * row_moment + 0.2 * row_full / D
    col_part = jnp.sum(squares, axis=0)
    sums = jnp.concatenate([col_part, jnp.full((128,), jnp.sum(row_moment_new))])
    sums = total_over(sums, ("zl", "core", "zh"))
    col_moment_new = 0.8 * col_moment + 0.2 * sums[:512] / FF
    row_average = sums[512] / FF
    update = gradient * lax.rsqrt(row_moment_new[:, None] * col_moment_new[None, :] / row_average)
    momentum_new = (0.9 * momentum.astype(jnp.float32) + 0.1 * update).astype(jnp.bfloat16)
    weights_new = weights - 0.01 * momentum_new.astype(jnp.float32)
    scores_new = scores - 50.0 * weights * gradient
    return (weights_new, momentum_new, scores_new, row_moment_new, col_moment_new)


def solution(mesh):
    fine = Mesh(mesh.devices.reshape(2, 2, 4, 4, 4), ("zl", "core", "x", "y", "zh"))
    dp, row, col = ("zl", "core"), ("x", "y"), "zh"
    return jax.shard_map(
        local,
        mesh=fine,
        in_specs=(
            P(dp, row),
            P(dp + row, col),
            P((col,) + dp, row),
            P((col,) + dp, row),
            P((col,) + dp, row),
            P((col,) + dp),
            P(row),
        ),
        out_specs=(
            P((col,) + dp, row),
            P((col,) + dp, row),
            P((col,) + dp, row),
            P((col,) + dp),
            P(row),
        ),
        check_vma=False,
    )
```

```python
import math

import jax
import jax.numpy as jnp
from jax import lax
from jax.experimental import pallas as pl
from jax.experimental.pallas import tpu as pltpu
from jax.sharding import Mesh, PartitionSpec as P

D = 8192
FF = 16384
CHUNKS = 4
STEPS = (0, -1, 1, 2)


def along_x(array, target):
    return lax.ppermute(array, "x", [(x, target(x)) for x in range(4)])


def along_y(array, step):
    return lax.ppermute(array, "y", [(y, (y + step) % 4) for y in range(4)])


def swap(array, axis):
    return lax.ppermute(array, axis, [(0, 1), (1, 0)])


def mate(x):
    return 3 - x


def partner(x):
    return x ^ 1


def far(x):
    return (x + 2) % 4


def x_step(own, other):
    return (own, along_x(own, mate), along_x(other, partner), along_x(other, far))


def y_gather(group, before):
    half = group.shape[0] // 2
    below = along_y(group, 1)
    above = along_y(group, -1)
    below, above, _ = lax.optimization_barrier((below, above, before))
    return group, below, above, along_y(below[:half], 1), along_y(above[half:], -1)


def product(grad_rows, act_rows):
    return lax.dot_general(
        grad_rows, act_rows, (((0,), (0,)), ((), ())), preferred_element_type=jnp.float32
    )


def token_sum(groups, acts):
    own, below, above, far_low, far_high = groups
    half = far_low.shape[0]
    total = product(own, acts[0]) + product(below, acts[1]) + product(above, acts[2])
    return total + product(far_low, acts[3][:half]) + product(far_high, acts[3][half:])


def spread(vector, axes):
    wide = jnp.broadcast_to(vector[None], (16, vector.shape[0]))
    return lax.all_to_all(wide, axes, 0, 0, tiled=True)


def step_kernel(kind, own, theirs, weights, momentum, scores, rows, cols, w_out, m_out, s_out):
    i = pl.program_id(0)
    here = i // (pl.num_programs(0) // 2) == kind[0]
    gradient = jnp.where(here, own[...], theirs[...].astype(jnp.float32))
    across = jnp.broadcast_to(rows[pl.ds(i, 1), :], (128, 128)).T
    across = jnp.concatenate([across] * 4, axis=1)
    update = gradient * (across * cols[...])
    moved = (0.9 * momentum[...].astype(jnp.float32) + 0.1 * update).astype(jnp.bfloat16)
    held = weights[...]
    m_out[...] = moved
    w_out[...] = held - 0.01 * moved.astype(jnp.float32)
    s_out[...] = scores[...] - 50.0 * held * gradient


def step(kind, own, theirs, weights, momentum, scores, rows, cols):
    steps = weights.shape[0] // 128
    half = pl.BlockSpec((128, 512), lambda i, kind: (i % (steps // 2), 0))
    block = pl.BlockSpec((128, 512), lambda i, kind: (i, 0))
    whole = lambda shape: pl.BlockSpec(shape, lambda i, kind: (0, 0))
    return pl.pallas_call(
        step_kernel,
        grid_spec=pltpu.PrefetchScalarGridSpec(
            num_scalar_prefetch=1,
            grid=(steps,),
            in_specs=[half, half, block, block, block, whole((steps, 128)), whole((1, 512))],
            out_specs=[block, block, block],
        ),
        out_shape=[
            jax.ShapeDtypeStruct(weights.shape, jnp.float32),
            jax.ShapeDtypeStruct(weights.shape, jnp.bfloat16),
            jax.ShapeDtypeStruct(weights.shape, jnp.float32),
        ],
    )(kind.reshape(1), own, theirs, weights, momentum, scores, rows.reshape(steps, 128), cols[None])


def local(activations, out_grads, weights, momentum, scores, row_moment, col_moment):
    token_scale = 1.0 / math.sqrt(activations.shape[0] * 4)
    core, low = lax.axis_index("core"), lax.axis_index("zl")
    x, y = lax.axis_index("x"), lax.axis_index("y")
    kind = (x ^ (x >> 1)) & 1

    rows = FF // 16
    half = rows // 2
    part = half // CHUNKS
    starts = [((low ^ a) * 2 + (core ^ b)) * rows for a in range(2) for b in range(2)]

    def columns(which, k):
        return jnp.concatenate(
            [
                lax.dynamic_slice_in_dim(out_grads, s + which * half + k * part, part, 1)
                for s in starts
            ],
            axis=1,
        )

    blocks = []
    for k in range(CHUNKS):
        own, other = columns(kind, k), columns(1 - kind, k)
        if k:
            own, other, *last = lax.optimization_barrier((own, other, *blocks[-1]))
            blocks[-1] = tuple(last)
        blocks.append(x_step(own, other))
        if k == 0:
            acts = activations.reshape(4, 4, 128, 512)
            order = (x, 3 - x, x ^ 1, 3 - (x ^ 1))
            acts = [
                jnp.concatenate(
                    [
                        lax.dynamic_slice(
                            acts, (i, (y + j) % 4, 0, 0), (1, 1, 128, 512)
                        ).reshape(128, 512)
                        for i in order
                    ],
                    axis=0,
                )
                for j in STEPS
            ]
            held, *last = lax.optimization_barrier((acts[0], *blocks[-1]))
            blocks[-1] = tuple(last)

    pair_acts = [along_x(held, partner)]
    for j in range(1, 4):
        held, pair_acts[-1] = lax.optimization_barrier((acts[j], pair_acts[-1]))
        pair_acts.append(along_x(held, partner))
    pair_turned = [jnp.concatenate([a[256:], a[:256]], axis=0) for a in pair_acts]

    own_parts, pair_parts, theirs = [], [], []
    core_seen, low_seen = (), ()
    for k in range(CHUNKS):
        groups = y_gather(jnp.concatenate(blocks[k], axis=0), pair_acts[k])
        own = token_sum(groups, acts).reshape(2, 2, part, 512)
        groups = lax.optimization_barrier((*groups, *core_seen[-1:], *low_seen[:-1][-1:]))[:5]
        pair = token_sum(groups, pair_turned).reshape(2, 2, part, 512)
        sent = swap(jnp.stack([own[:, 1], pair[:, 1]]).astype(jnp.bfloat16), "core")
        core_seen += (sent,)
        chip_own = own[:, 0] + sent[0].astype(jnp.float32)
        chip_pair = pair[:, 0] + sent[1].astype(jnp.float32)
        sent = swap(jnp.stack([chip_own[1], chip_pair[1]]).astype(jnp.bfloat16), "zl")
        low_seen += (sent,)
        own_parts.append((chip_own[0] + sent[0].astype(jnp.float32)) * token_scale)
        pair_parts.append((chip_pair[0] + sent[1].astype(jnp.float32)) * token_scale)
        theirs.append(along_x(pair_parts[-1].astype(jnp.bfloat16), partner))
    row_part = jnp.concatenate(
        [
            jnp.sum(a * a + 1e-30, axis=1) + jnp.sum(b * b + 1e-30, axis=1)
            for a, b in zip(own_parts, pair_parts)
        ]
    )
    row_parts = spread(row_part, ("x", "y"))
    row_parts, *theirs = lax.optimization_barrier((row_parts, *theirs))
    row_parts = row_parts.reshape(4, 4, half)
    row_full = jnp.concatenate(
        [jnp.sum(row_parts[0] + row_parts[3], axis=0), jnp.sum(row_parts[1] + row_parts[2], axis=0)]
    )
    row_moment_new = 0.8 * row_moment + 0.2 * row_full / D
    col_part = sum(jnp.sum(a * a + 1e-30, axis=0) for a in own_parts)
    for a in theirs:
        wide = a.astype(jnp.float32)
        col_part = col_part + jnp.sum(wide * wide + 1e-30, axis=0)
    sums = jnp.concatenate([col_part, jnp.full((128,), jnp.sum(row_moment_new))])
    sums = jnp.sum(spread(sums, ("zl", "core", "zh")), axis=0)
    col_moment_new = 0.8 * col_moment + 0.2 * sums[:512] / FF
    row_average = sums[512] / FF
    outs = step(
        kind,
        jnp.concatenate(own_parts, axis=0),
        jnp.concatenate(theirs, axis=0),
        weights,
        momentum,
        scores,
        lax.rsqrt(row_moment_new),
        lax.rsqrt(col_moment_new / row_average),
    )
    return (*outs, row_moment_new, col_moment_new)


def solution(mesh):
    fine = Mesh(mesh.devices.reshape(2, 2, 4, 4, 4), ("zl", "core", "x", "y", "zh"))
    dp, row, col = ("zl", "core"), ("x", "y"), "zh"
    return jax.shard_map(
        local,
        mesh=fine,
        in_specs=(
            P(dp, row),
            P(dp + row, col),
            P((col,) + dp, row),
            P((col,) + dp, row),
            P((col,) + dp, row),
            P((col,) + dp),
            P(row),
        ),
        out_specs=(
            P((col,) + dp, row),
            P((col,) + dp, row),
            P((col,) + dp, row),
            P((col,) + dp),
            P(row),
        ),
        check_vma=False,
    )
```

```python
import math

import jax
import jax.numpy as jnp
from jax import lax
from jax.sharding import Mesh, PartitionSpec as P

D = 8192
FF = 16384
AXES = ("core", "x", "y")
STEPS = (0, -1, 1, 2)


def ring_pairs(phase, step):
    pairs = []
    for core in range(2):
        for x in range(4):
            for y in range(4):
                if core == phase:
                    to = (x + step) % 4 * 4 + y
                else:
                    to = x * 4 + (y + step) % 4
                pairs.append((core * 16 + x * 4 + y, core * 16 + to))
    return pairs


def shift(array, phase, step):
    return lax.ppermute(array, AXES, ring_pairs(phase, step))


def along_z(array, step):
    place = lambda z: z % 2 * 4 + z // 2
    return lax.ppermute(array, ("zl", "zh"), [(place(z), place((z + step) % 8)) for z in range(8)])


def swap(array, axis):
    return lax.ppermute(array, axis, [(0, 1), (1, 0)])


def ring_start(block, phase):
    return [block, shift(block, phase, 1), shift(block, phase, -1)]


def ring_end(blocks, phase):
    block, below, above = blocks
    half = block.shape[0] // 2
    return [*blocks, shift(below[:half], phase, 1), shift(above[half:], phase, -1)]


def after(blocks, *others):
    return lax.optimization_barrier((*blocks, *others))[: len(blocks)]


def product(grad_rows, act_rows):
    return lax.dot_general(
        grad_rows, act_rows, (((0,), (0,)), ((), ())), preferred_element_type=jnp.float32
    )


def token_sum(groups, acts):
    own, below, above, far_low, far_high = groups
    half = far_low.shape[0]
    total = product(own, acts[0]) + product(below, acts[1]) + product(above, acts[2])
    return total + product(far_low, acts[3][:half]) + product(far_high, acts[3][half:])


def total_over(vector, axes):
    spread = jnp.broadcast_to(vector[None], (16, vector.shape[0]))
    return jnp.sum(lax.all_to_all(spread, axes, 0, 0, tiled=True), axis=0)


def local(activations, out_grads, weights, momentum, scores, row_moment, col_moment):
    token_scale = 1.0 / math.sqrt(activations.shape[0] * 4)
    core, low = lax.axis_index("core"), lax.axis_index("zl")
    x, y = lax.axis_index("x"), lax.axis_index("y")
    rows = FF // 16

    def units(a, b):
        return lax.dynamic_slice_in_dim(out_grads, ((low ^ a) * 2 + (core ^ b)) * rows, rows, 1)

    other = swap(jnp.concatenate([units(0, 1), units(1, 1)], axis=0), "core")
    tokens = other.shape[0] // 2
    near = jnp.concatenate([units(0, 0), other[:tokens]], axis=0)
    away = swap(jnp.concatenate([units(1, 0), other[tokens:]], axis=0), "zl")

    half = activations.shape[0] // 2
    acts_core = swap(activations, "core")
    acts_below, acts_above = along_z(activations[:half], 1), along_z(activations[half:], -1)

    def arranged(first, second):
        first, second = (a.reshape(16, tokens, -1) for a in (first, second))
        groups = []
        for j in STEPS:
            parts = []
            for i in STEPS:
                at = jnp.where(
                    core == 0, (x + i) % 4 * 4 + (y + j) % 4, (x + j) % 4 * 4 + (y + i) % 4
                )
                parts += [lax.dynamic_index_in_dim(a, at, 0, False) for a in (first, second)]
            groups.append(jnp.concatenate(parts, axis=0))
        return groups

    near = ring_end(ring_start(near, 0), 0)
    near = ring_start(jnp.concatenate(after(near, away), axis=0), 1)
    away = ring_end(ring_start(away, 0), 0)
    groups_near = ring_end(after(near, *away), 1)
    groups_away = ring_end(ring_start(jnp.concatenate(away, axis=0), 1), 1)
    acts_below, acts_above = after((acts_below, acts_above), *groups_near[3:])
    acts_low = jnp.concatenate([acts_below, acts_above], axis=0)
    acts_both = swap(acts_low, "core")
    gradient = token_sum(groups_near, arranged(activations, acts_core))
    gradient = gradient + token_sum(groups_away, arranged(acts_low, acts_both))
    gradient = gradient * token_scale

    squares = gradient * gradient + 1e-30
    row_full = total_over(jnp.sum(squares, axis=1), ("x", "y"))
    row_moment_new = 0.8 * row_moment + 0.2 * row_full / D
    col_part = jnp.sum(squares, axis=0)
    sums = jnp.concatenate([col_part, jnp.full((128,), jnp.sum(row_moment_new))])
    sums = total_over(sums, ("zl", "core", "zh"))
    col_moment_new = 0.8 * col_moment + 0.2 * sums[:512] / FF
    row_average = sums[512] / FF
    update = gradient * lax.rsqrt(row_moment_new[:, None] * col_moment_new[None, :] / row_average)
    momentum_new = (0.9 * momentum.astype(jnp.float32) + 0.1 * update).astype(jnp.bfloat16)
    weights_new = weights - 0.01 * momentum_new.astype(jnp.float32)
    scores_new = scores - 50.0 * weights * gradient
    return (weights_new, momentum_new, scores_new, row_moment_new, col_moment_new)


def solution(mesh):
    fine = Mesh(mesh.devices.reshape(2, 2, 4, 4, 4), ("zl", "core", "x", "y", "zh"))
    dp, row, col = ("zl", "core"), ("x", "y"), "zh"
    return jax.shard_map(
        local,
        mesh=fine,
        in_specs=(
            P(dp, row),
            P(dp + row, col),
            P((col,) + dp, row),
            P((col,) + dp, row),
            P((col,) + dp, row),
            P((col,) + dp),
            P(row),
        ),
        out_specs=(
            P((col,) + dp, row),
            P((col,) + dp, row),
            P((col,) + dp, row),
            P((col,) + dp),
            P(row),
        ),
        check_vma=False,
    )
```

```python
import math

import jax
import jax.numpy as jnp
from jax import lax
from jax.experimental import pallas as pl
from jax.experimental.pallas import tpu as pltpu
from jax.sharding import Mesh, PartitionSpec as P

D = 8192
FF = 16384
AXES = ("core", "x", "y")
STEPS = (0, -1, 1, 2)


def ring_pairs(phase, step):
    pairs = []
    for core in range(2):
        for x in range(4):
            for y in range(4):
                if core == phase:
                    to = (x + step) % 4 * 4 + y
                else:
                    to = x * 4 + (y + step) % 4
                pairs.append((core * 16 + x * 4 + y, core * 16 + to))
    return pairs


def shift(array, phase, step):
    return lax.ppermute(array, AXES, ring_pairs(phase, step))


def along_z(array, step):
    place = lambda z: z % 2 * 4 + z // 2
    return lax.ppermute(array, ("zl", "zh"), [(place(z), place((z + step) % 8)) for z in range(8)])


def swap(array, axis):
    return lax.ppermute(array, axis, [(0, 1), (1, 0)])


def first_ring(block):
    return [block, shift(block, 0, 1), shift(block, 0, -1), shift(block, 0, 2)]


def second_start(block):
    return [block, shift(block, 1, 1), shift(block, 1, -1)]


def second_end(blocks):
    block, below, above = blocks
    half = block.shape[0] // 2
    return [*blocks, shift(below[:half], 1, 1), shift(above[half:], 1, -1)]


def product(grad_rows, act_rows):
    return lax.dot_general(
        grad_rows, act_rows, (((0,), (0,)), ((), ())), preferred_element_type=jnp.float32
    )


def add_products(total, groups, acts):
    half = groups[3].shape[0]
    for rows, cols in zip(groups, (*acts[:3], acts[3][:half], acts[3][half:])):
        term = product(rows, cols)
        total = term if total is None else total + term
    return total


def arrange_kernel(place, first, second, out):
    tokens = first.shape[0]
    out[:tokens] = first[...]
    out[tokens:] = second[...]


def arranged(places, first, second, tokens):
    block = pl.BlockSpec((tokens, first.shape[1]), lambda i, place: (place[i], 0))
    out = pl.pallas_call(
        arrange_kernel,
        grid_spec=pltpu.PrefetchScalarGridSpec(
            num_scalar_prefetch=1,
            grid=(16,),
            in_specs=[block, block],
            out_specs=pl.BlockSpec((2 * tokens, first.shape[1]), lambda i, place: (i, 0)),
        ),
        out_shape=jax.ShapeDtypeStruct((32 * tokens, first.shape[1]), first.dtype),
        cost_estimate=pl.CostEstimate(
            flops=0, bytes_accessed=128 * tokens * first.shape[1], transcendentals=0
        ),
    )(places, first, second)
    return out.reshape(4, 8 * tokens, first.shape[1])


def total_over(vector, axes):
    spread = jnp.broadcast_to(vector[None], (16, vector.shape[0]))
    return jnp.sum(lax.all_to_all(spread, axes, 0, 0, tiled=True), axis=0)


def local(activations, out_grads, weights, momentum, scores, row_moment, col_moment):
    token_scale = 1.0 / math.sqrt(activations.shape[0] * 4)
    core, low = lax.axis_index("core"), lax.axis_index("zl")
    x, y = lax.axis_index("x"), lax.axis_index("y")
    rows = FF // 16

    def units(a, b):
        return lax.dynamic_slice_in_dim(out_grads, ((low ^ a) * 2 + (core ^ b)) * rows, rows, 1)

    other = swap(jnp.concatenate([units(0, 1), units(1, 1)], axis=0), "core")
    tokens = other.shape[0] // 2
    near = jnp.concatenate([units(0, 0), other[:tokens]], axis=0)
    away = jnp.concatenate([units(1, 0), other[tokens:]], axis=0)
    acts_core = swap(activations, "core")

    places = []
    for j in STEPS:
        for i in STEPS:
            dx, dy = jnp.where(core == 0, i, j), jnp.where(core == 0, j, i)
            places.append((x + dx) % 4 * 4 + (y + dy) % 4)
    places = jnp.stack(places).astype(jnp.int32)

    *near, acts_core, away, sent = lax.optimization_barrier(
        (*first_ring(near), acts_core, away, activations)
    )
    near = second_start(jnp.concatenate(near, axis=0))
    away = swap(away, "zl")
    half = sent.shape[0] // 2
    acts_below, acts_above = along_z(sent[:half], 1), along_z(sent[half:], -1)
    away, acts_below, acts_above = lax.optimization_barrier((away, acts_below, acts_above))
    *away, acts_below, acts_above = lax.optimization_barrier(
        (*first_ring(away), acts_below, acts_above)
    )
    away = second_start(jnp.concatenate(away, axis=0))
    near = second_end(near)
    gradient = add_products(None, near, arranged(places, activations, acts_core, tokens))
    acts_low = jnp.concatenate([acts_below, acts_above], axis=0)
    acts_away = arranged(places, acts_low, swap(acts_low, "core"), tokens)
    *away, acts_away, gradient = lax.optimization_barrier((*away, acts_away, gradient))
    gradient = add_products(gradient, second_end(away), acts_away)
    gradient = gradient * token_scale

    squares = gradient * gradient + 1e-30
    row_full = total_over(jnp.sum(squares, axis=1), ("x", "y"))
    row_moment_new = 0.8 * row_moment + 0.2 * row_full / D
    col_part = jnp.sum(squares, axis=0)
    sums = jnp.concatenate([col_part, jnp.sum(row_moment_new.reshape(8, 128), axis=0)])
    sums = total_over(sums, ("zl", "core", "zh"))
    col_moment_new = 0.8 * col_moment + 0.2 * sums[:512] / FF
    row_average = jnp.sum(sums[512:]) / FF
    update = gradient * lax.rsqrt(row_moment_new[:, None] * col_moment_new[None, :] / row_average)
    momentum_new = (0.9 * momentum.astype(jnp.float32) + 0.1 * update).astype(jnp.bfloat16)
    weights_new = weights - 0.01 * momentum_new.astype(jnp.float32)
    scores_new = scores - 50.0 * weights * gradient
    return (weights_new, momentum_new, scores_new, row_moment_new, col_moment_new)


def solution(mesh):
    fine = Mesh(mesh.devices.reshape(2, 2, 4, 4, 4), ("zl", "core", "x", "y", "zh"))
    dp, row, col = ("zl", "core"), ("x", "y"), "zh"
    return jax.shard_map(
        local,
        mesh=fine,
        in_specs=(
            P(dp, row),
            P(dp + row, col),
            P((col,) + dp, row),
            P((col,) + dp, row),
            P((col,) + dp, row),
            P((col,) + dp),
            P(row),
        ),
        out_specs=(
            P((col,) + dp, row),
            P((col,) + dp, row),
            P((col,) + dp, row),
            P((col,) + dp),
            P(row),
        ),
        check_vma=False,
    )
```

```python
import math

import jax
import jax.numpy as jnp
from jax import lax
from jax.experimental import pallas as pl
from jax.experimental.pallas import tpu as pltpu
from jax.sharding import Mesh, PartitionSpec as P

D = 8192
FF = 16384
AXES = ("core", "x", "y")
STEPS = (0, -1, 1, 2)


def ring_pairs(phase, step):
    pairs = []
    for core in range(2):
        for x in range(4):
            for y in range(4):
                if core == phase:
                    to = (x + step) % 4 * 4 + y
                else:
                    to = x * 4 + (y + step) % 4
                pairs.append((core * 16 + x * 4 + y, core * 16 + to))
    return pairs


def shift(array, phase, step):
    return lax.ppermute(array, AXES, ring_pairs(phase, step))


def along_z(array, step):
    place = lambda z: z % 2 * 4 + z // 2
    return lax.ppermute(array, ("zl", "zh"), [(place(z), place((z + step) % 8)) for z in range(8)])


def swap(array, axis):
    return lax.ppermute(array, axis, [(0, 1), (1, 0)])


def ring_start(block, phase):
    return [block, shift(block, phase, 1), shift(block, phase, -1)]


def ring_end(blocks, phase, step):
    return [*blocks, shift(blocks[1] if step == 1 else blocks[2], phase, step)]


def after(blocks, *others):
    return lax.optimization_barrier((*blocks, *others))[: len(blocks)]


def product(grad_rows, act_rows):
    return lax.dot_general(
        grad_rows, act_rows, (((0,), (0,)), ((), ())), preferred_element_type=jnp.float32
    )


def arrange_kernel(place, first, second, out, sems):
    tokens = first.shape[0] // 16
    copies = []
    for i in range(16):
        rows = pl.ds(pl.multiple_of(place[i] * tokens, tokens), tokens)
        for c, source in enumerate((first, second)):
            at = pl.ds((2 * i + c) * tokens, tokens)
            copies.append(pltpu.make_async_copy(source.at[rows], out.at[at], sems.at[2 * i + c]))
    for copy in copies:
        copy.start()
    for copy in copies:
        copy.wait()


def arranged(places, first, second):
    rows, width = first.shape
    anywhere = pl.BlockSpec(memory_space=pl.ANY)
    out = pl.pallas_call(
        arrange_kernel,
        in_specs=[pl.BlockSpec(memory_space=pltpu.SMEM), anywhere, anywhere],
        out_specs=anywhere,
        out_shape=jax.ShapeDtypeStruct((2 * rows, width), first.dtype),
        scratch_shapes=[pltpu.SemaphoreType.DMA((32,))],
        cost_estimate=pl.CostEstimate(
            flops=0, bytes_accessed=8 * rows * width, transcendentals=0
        ),
    )(places, first, second)
    return out.reshape(4, rows // 2, width)


def total_over(vector, axes):
    spread = jnp.broadcast_to(vector[None], (16, vector.shape[0]))
    return jnp.sum(lax.all_to_all(spread, axes, 0, 0, tiled=True), axis=0)


def local(activations, out_grads, weights, momentum, scores, row_moment, col_moment):
    token_scale = 1.0 / math.sqrt(activations.shape[0] * 4)
    core, low = lax.axis_index("core"), lax.axis_index("zl")
    x, y = lax.axis_index("x"), lax.axis_index("y")
    rows = FF // 16

    def units(a, b):
        return lax.dynamic_slice_in_dim(out_grads, ((low ^ a) * 2 + (core ^ b)) * rows, rows, 1)

    other = swap(jnp.concatenate([units(0, 1), units(1, 1)], axis=0), "core")
    tokens = other.shape[0] // 2
    near = jnp.concatenate([units(0, 0), other[:tokens]], axis=0)
    away = swap(jnp.concatenate([units(1, 0), other[tokens:]], axis=0), "zl")
    acts_core = swap(activations, "core")

    places = []
    for j in STEPS:
        for i in STEPS:
            dx, dy = jnp.where(core == 0, i, j), jnp.where(core == 0, j, i)
            places.append((x + dx) % 4 * 4 + (y + dy) % 4)
    places = jnp.stack(places).astype(jnp.int32)

    near = after(ring_end(ring_start(near, 0), 0, 1), away)
    (sent,) = after((activations,), *near)
    near = ring_start(jnp.concatenate(near, axis=0), 1)
    away = ring_end(ring_start(away, 0), 0, -1)
    half = sent.shape[0] // 2
    acts_low = (along_z(sent[:half], 1), along_z(sent[half:], -1))
    first = arranged(places, activations, acts_core)
    gradient = product(near[0], first[0]) + product(near[1], first[1]) + product(near[2], first[2])
    near = ring_end(after(near, *away), 1, 1)
    away = ring_start(jnp.concatenate(away, axis=0), 1)
    away[2], gradient = lax.optimization_barrier((away[2], gradient))
    away = ring_end(away, 1, -1)
    acts_low = jnp.concatenate(after(acts_low, away[2]), axis=0)
    second = arranged(places, acts_low, swap(acts_low, "core"))
    gradient = gradient + product(near[3], first[3])
    gradient = gradient + product(away[0], second[0]) + product(away[2], second[2])
    last = lax.optimization_barrier((product(away[1], second[1]), product(away[3], second[3])))
    gradient = gradient + (last[0] + last[1])
    gradient = gradient * token_scale

    squares = gradient * gradient + 1e-30
    row_full = total_over(jnp.sum(squares, axis=1), ("x", "y"))
    row_moment_new = 0.8 * row_moment + 0.2 * row_full / D
    col_part = jnp.sum(squares, axis=0)
    sums = jnp.concatenate([col_part, jnp.sum(row_moment_new.reshape(8, 128), axis=0)])
    sums = total_over(sums, ("zl", "core", "zh"))
    col_moment_new = 0.8 * col_moment + 0.2 * sums[:512] / FF
    row_average = jnp.sum(sums[512:]) / FF
    update = gradient * lax.rsqrt(row_moment_new[:, None] * col_moment_new[None, :] / row_average)
    momentum_new = (0.9 * momentum.astype(jnp.float32) + 0.1 * update).astype(jnp.bfloat16)
    weights_new = weights - 0.01 * momentum_new.astype(jnp.float32)
    scores_new = scores - 50.0 * weights * gradient
    return (weights_new, momentum_new, scores_new, row_moment_new, col_moment_new)


def solution(mesh):
    fine = Mesh(mesh.devices.reshape(2, 2, 4, 4, 4), ("zl", "core", "x", "y", "zh"))
    dp, row, col = ("zl", "core"), ("x", "y"), "zh"
    return jax.shard_map(
        local,
        mesh=fine,
        in_specs=(
            P(dp, row),
            P(dp + row, col),
            P((col,) + dp, row),
            P((col,) + dp, row),
            P((col,) + dp, row),
            P((col,) + dp),
            P(row),
        ),
        out_specs=(
            P((col,) + dp, row),
            P((col,) + dp, row),
            P((col,) + dp, row),
            P((col,) + dp),
            P(row),
        ),
        check_vma=False,
    )
```

```python
import math

import jax
import jax.numpy as jnp
from jax import lax
from jax.experimental import pallas as pl
from jax.experimental.pallas import tpu as pltpu
from jax.sharding import Mesh, PartitionSpec as P

D = 8192
FF = 16384
AXES = ("core", "x", "y")
STEPS = (0, -1, 1, 2)


def ring_pairs(phase, step):
    pairs = []
    for core in range(2):
        for x in range(4):
            for y in range(4):
                if core == phase:
                    to = (x + step) % 4 * 4 + y
                else:
                    to = x * 4 + (y + step) % 4
                pairs.append((core * 16 + x * 4 + y, core * 16 + to))
    return pairs


def shift(array, phase, step):
    return lax.ppermute(array, AXES, ring_pairs(phase, step))


def along_z(array, step):
    place = lambda z: z % 2 * 4 + z // 2
    return lax.ppermute(array, ("zl", "zh"), [(place(z), place((z + step) % 8)) for z in range(8)])


def swap(array, axis):
    return lax.ppermute(array, axis, [(0, 1), (1, 0)])


def ring_start(block, phase):
    return [block, shift(block, phase, 1), shift(block, phase, -1)]


def ring_end(blocks, phase, step):
    return [*blocks, shift(blocks[1] if step == 1 else blocks[2], phase, step)]


def after(blocks, *others):
    return lax.optimization_barrier((*blocks, *others))[: len(blocks)]


def product(grad_rows, act_rows):
    return lax.dot_general(
        grad_rows, act_rows, (((0,), (0,)), ((), ())), preferred_element_type=jnp.float32
    )


def arrange_kernel(place, first, second, out, sems):
    tokens = first.shape[0] // 16
    copies = []
    for i in range(16):
        rows = pl.ds(pl.multiple_of(place[i] * tokens, tokens), tokens)
        for c, source in enumerate((first, second)):
            at = pl.ds((2 * i + c) * tokens, tokens)
            copies.append(pltpu.make_async_copy(source.at[rows], out.at[at], sems.at[2 * i + c]))
    for copy in copies:
        copy.start()
    for copy in copies:
        copy.wait()


def arranged(places, first, second):
    rows, width = first.shape
    anywhere = pl.BlockSpec(memory_space=pl.ANY)
    out = pl.pallas_call(
        arrange_kernel,
        in_specs=[pl.BlockSpec(memory_space=pltpu.SMEM), anywhere, anywhere],
        out_specs=pl.BlockSpec(memory_space=pltpu.VMEM),
        out_shape=jax.ShapeDtypeStruct((2 * rows, width), first.dtype),
        scratch_shapes=[pltpu.SemaphoreType.DMA((32,))],
        compiler_params=pltpu.CompilerParams(vmem_limit_bytes=8 << 20),
        cost_estimate=pl.CostEstimate(
            flops=0, bytes_accessed=8 * rows * width, transcendentals=0
        ),
    )(places, first, second)
    return out.reshape(4, rows // 2, width)


def total_over(vector, axes):
    spread = jnp.broadcast_to(vector[None], (16, vector.shape[0]))
    return jnp.sum(lax.all_to_all(spread, axes, 0, 0, tiled=True), axis=0)


def local(activations, out_grads, weights, momentum, scores, row_moment, col_moment):
    token_scale = 1.0 / math.sqrt(activations.shape[0] * 4)
    core, low = lax.axis_index("core"), lax.axis_index("zl")
    x, y = lax.axis_index("x"), lax.axis_index("y")
    rows = FF // 16

    def units(a, b):
        return lax.dynamic_slice_in_dim(out_grads, ((low ^ a) * 2 + (core ^ b)) * rows, rows, 1)

    other = swap(jnp.concatenate([units(0, 1), units(1, 1)], axis=0), "core")
    tokens = other.shape[0] // 2
    near = jnp.concatenate([units(0, 0), other[:tokens]], axis=0)
    away = swap(jnp.concatenate([units(1, 0), other[tokens:]], axis=0), "zl")
    acts_core = swap(activations, "core")

    places = []
    for j in STEPS:
        for i in STEPS:
            dx, dy = jnp.where(core == 0, i, j), jnp.where(core == 0, j, i)
            places.append((x + dx) % 4 * 4 + (y + dy) % 4)
    places = jnp.stack(places).astype(jnp.int32)

    near = after(ring_end(ring_start(near, 0), 0, 1), away)
    (sent,) = after((activations,), *near)
    near = ring_start(jnp.concatenate(near, axis=0), 1)
    away = ring_end(ring_start(away, 0), 0, -1)
    half = sent.shape[0] // 2
    acts_low = (along_z(sent[:half], 1), along_z(sent[half:], -1))
    first = arranged(places, activations, acts_core)
    gradient = product(near[0], first[0]) + product(near[1], first[1]) + product(near[2], first[2])
    near = ring_end(after(near, *away), 1, 1)
    away = ring_start(jnp.concatenate(away, axis=0), 1)
    away[2], gradient = lax.optimization_barrier((away[2], gradient))
    away = ring_end(away, 1, -1)
    acts_low = jnp.concatenate(after(acts_low, away[2]), axis=0)
    second = arranged(places, acts_low, swap(acts_low, "core"))
    gradient = gradient + product(near[3], first[3])
    gradient = gradient + product(away[0], second[0]) + product(away[2], second[2])
    last = lax.optimization_barrier((product(away[1], second[1]), product(away[3], second[3])))
    gradient = gradient + (last[0] + last[1])
    gradient = gradient * token_scale

    squares = gradient * gradient + 1e-30
    row_full = total_over(jnp.sum(squares, axis=1), ("x", "y"))
    row_moment_new = 0.8 * row_moment + 0.2 * row_full / D
    col_part = jnp.sum(squares, axis=0)
    sums = jnp.concatenate([col_part, jnp.sum(row_moment_new.reshape(8, 128), axis=0)])
    sums = total_over(sums, ("zl", "core", "zh"))
    col_moment_new = 0.8 * col_moment + 0.2 * sums[:512] / FF
    row_average = jnp.sum(sums[512:]) / FF
    update = gradient * lax.rsqrt(row_moment_new[:, None] * col_moment_new[None, :] / row_average)
    momentum_new = (0.9 * momentum.astype(jnp.float32) + 0.1 * update).astype(jnp.bfloat16)
    weights_new = weights - 0.01 * momentum_new.astype(jnp.float32)
    scores_new = scores - 50.0 * weights * gradient
    return (weights_new, momentum_new, scores_new, row_moment_new, col_moment_new)


def solution(mesh):
    fine = Mesh(mesh.devices.reshape(2, 2, 4, 4, 4), ("zl", "core", "x", "y", "zh"))
    dp, row, col = ("zl", "core"), ("x", "y"), "zh"
    return jax.shard_map(
        local,
        mesh=fine,
        in_specs=(
            P(dp, row),
            P(dp + row, col),
            P((col,) + dp, row),
            P((col,) + dp, row),
            P((col,) + dp, row),
            P((col,) + dp),
            P(row),
        ),
        out_specs=(
            P((col,) + dp, row),
            P((col,) + dp, row),
            P((col,) + dp, row),
            P((col,) + dp),
            P(row),
        ),
        check_vma=False,
    )
```

```python
import math

import jax
import jax.numpy as jnp
from jax import lax
from jax.experimental import pallas as pl
from jax.experimental.pallas import tpu as pltpu
from jax.sharding import Mesh, PartitionSpec as P

D = 8192
FF = 16384
AXES = ("core", "x", "y")
STEPS = (0, -1, 1, 2)


def ring_pairs(phase, step):
    pairs = []
    for core in range(2):
        for x in range(4):
            for y in range(4):
                if core == phase:
                    to = (x + step) % 4 * 4 + y
                else:
                    to = x * 4 + (y + step) % 4
                pairs.append((core * 16 + x * 4 + y, core * 16 + to))
    return pairs


def shift(array, phase, step):
    return lax.ppermute(array, AXES, ring_pairs(phase, step))


def along_z(array, step):
    place = lambda z: z % 2 * 4 + z // 2
    return lax.ppermute(array, ("zl", "zh"), [(place(z), place((z + step) % 8)) for z in range(8)])


def swap(array, axis):
    return lax.ppermute(array, axis, [(0, 1), (1, 0)])


def ring_start(block, phase):
    return [block, *lax.optimization_barrier((shift(block, phase, 1), shift(block, phase, -1)))]


def ring_up(blocks, phase):
    return [*blocks, shift(blocks[1], phase, 1)]


def ring_both(blocks, phase):
    half = blocks[0].shape[0] // 2
    return [*blocks, shift(blocks[1][:half], phase, 1), shift(blocks[2][half:], phase, -1)]


def after(blocks, *others):
    return lax.optimization_barrier((*blocks, *others))[: len(blocks)]


def product(grad_rows, act_rows):
    return lax.dot_general(
        grad_rows, act_rows, (((0,), (0,)), ((), ())), preferred_element_type=jnp.float32
    )


def arrange_kernel(place, *refs):
    *sources, out, sems = refs
    tokens = sources[0].shape[0] // 16
    copies = []
    for i in range(16):
        rows = pl.ds(pl.multiple_of(place[i] * tokens, tokens), tokens)
        for source in sources:
            at = pl.ds(len(copies) * tokens, tokens)
            copies.append(
                pltpu.make_async_copy(source.at[rows], out.at[at], sems.at[len(copies)])
            )
    for copy in copies:
        copy.start()
    for copy in copies:
        copy.wait()


def arranged(places, *sources):
    rows, width = sources[0].shape
    rows *= len(sources)
    size = rows * width * 2
    out = pl.pallas_call(
        arrange_kernel,
        in_specs=[pl.BlockSpec(memory_space=pltpu.SMEM)]
        + [pl.BlockSpec(memory_space=pl.ANY)] * len(sources),
        out_specs=pl.BlockSpec(memory_space=pltpu.VMEM),
        out_shape=jax.ShapeDtypeStruct((rows, width), sources[0].dtype),
        scratch_shapes=[pltpu.SemaphoreType.DMA((16 * len(sources),))],
        compiler_params=pltpu.CompilerParams(vmem_limit_bytes=size + (2 << 20)),
        cost_estimate=pl.CostEstimate(flops=0, bytes_accessed=2 * size, transcendentals=0),
    )(places, *sources)
    return out.reshape(4, rows // 4, width)


def total_over(vector, axes):
    spread = jnp.broadcast_to(vector[None], (16, vector.shape[0]))
    return jnp.sum(lax.all_to_all(spread, axes, 0, 0, tiled=True), axis=0)


def local(activations, out_grads, weights, momentum, scores, row_moment, col_moment):
    token_scale = 1.0 / math.sqrt(activations.shape[0] * 4)
    core, low = lax.axis_index("core"), lax.axis_index("zl")
    x, y = lax.axis_index("x"), lax.axis_index("y")
    rows = FF // 16

    def units(a, b):
        return lax.dynamic_slice_in_dim(out_grads, ((low ^ a) * 2 + (core ^ b)) * rows, rows, 1)

    near = units(0, 0)
    other = swap(jnp.concatenate([units(0, 1), units(1, 1)], axis=0), "core")
    tokens = near.shape[0]
    away = swap(jnp.concatenate([units(1, 0), other[tokens:]], axis=0), "zl")
    away = jnp.concatenate([other[:tokens], away], axis=0)
    acts_core = swap(activations, "core")

    places = []
    for j in STEPS:
        for i in STEPS:
            dx, dy = jnp.where(core == 0, i, j), jnp.where(core == 0, j, i)
            places.append((x + dx) % 4 * 4 + (y + dy) % 4)
    places = jnp.stack(places).astype(jnp.int32)

    near = ring_up(ring_start(near, 0), 0)
    near[3], away, sent = lax.optimization_barrier((near[3], away, activations))
    near = ring_start(jnp.concatenate(near, axis=0), 1)
    away = ring_both(ring_start(away, 0), 0)
    half = sent.shape[0] // 2
    acts_low = (along_z(sent[:half], 1), along_z(sent[half:], -1))
    near = ring_up(near, 1)
    away = ring_start(jnp.concatenate(away, axis=0), 1)
    first = arranged(places, activations)
    gradient = product(near[0], first[0])
    for k in (2, 1, 3):
        gradient = gradient + product(near[k], first[k])
    acts_low = jnp.concatenate(after(acts_low, near[3]), axis=0)
    second = arranged(places, acts_core, acts_low, swap(acts_low, "core"))
    gradient = gradient + product(away[0], second[0])
    *away, gradient = lax.optimization_barrier((*away, gradient))
    away = ring_both(away, 1)
    half = away[3].shape[0]
    gradient = gradient + product(away[1], second[1]) + product(away[2], second[2])
    last = (product(away[3], second[3][:half]), product(away[4], second[3][half:]))
    last = lax.optimization_barrier(last)
    gradient = gradient + (last[0] + last[1])
    gradient = gradient * token_scale

    squares = gradient * gradient + 1e-30
    row_full = total_over(jnp.sum(squares, axis=1), ("x", "y"))
    row_moment_new = 0.8 * row_moment + 0.2 * row_full / D
    col_part = jnp.sum(squares, axis=0)
    sums = jnp.concatenate([col_part, jnp.sum(row_moment_new.reshape(8, 128), axis=0)])
    scores_new = scores - 50.0 * weights * gradient
    sums = total_over(sums, ("zl", "core", "zh"))
    sums, weights, gradient = lax.optimization_barrier((sums, weights, gradient))
    col_moment_new = 0.8 * col_moment + 0.2 * sums[:512] / FF
    row_average = jnp.sum(sums[512:]) / FF
    scale = lax.rsqrt(row_moment_new)[:, None] * lax.rsqrt(col_moment_new / row_average)[None, :]
    momentum_new = (0.9 * momentum.astype(jnp.float32) + 0.1 * (gradient * scale)).astype(jnp.bfloat16)
    weights_new = weights - 0.01 * momentum_new.astype(jnp.float32)
    return (weights_new, momentum_new, scores_new, row_moment_new, col_moment_new)


def solution(mesh):
    fine = Mesh(mesh.devices.reshape(2, 2, 4, 4, 4), ("zl", "core", "x", "y", "zh"))
    dp, row, col = ("zl", "core"), ("x", "y"), "zh"
    return jax.shard_map(
        local,
        mesh=fine,
        in_specs=(
            P(dp, row),
            P(dp + row, col),
            P((col,) + dp, row),
            P((col,) + dp, row),
            P((col,) + dp, row),
            P((col,) + dp),
            P(row),
        ),
        out_specs=(
            P((col,) + dp, row),
            P((col,) + dp, row),
            P((col,) + dp, row),
            P((col,) + dp),
            P(row),
        ),
        check_vma=False,
    )
```

```python
import math

import jax
import jax.numpy as jnp
from jax import lax
from jax.experimental import pallas as pl
from jax.experimental.pallas import tpu as pltpu
from jax.sharding import Mesh, PartitionSpec as P

D = 8192
FF = 16384
AXES = ("core", "x", "y")
STEPS = (0, -1, 1, 2)


def ring_pairs(phase, step):
    pairs = []
    for core in range(2):
        for x in range(4):
            for y in range(4):
                if core == phase:
                    to = (x + step) % 4 * 4 + y
                else:
                    to = x * 4 + (y + step) % 4
                pairs.append((core * 16 + x * 4 + y, core * 16 + to))
    return pairs


def shift(array, phase, step):
    return lax.ppermute(array, AXES, ring_pairs(phase, step))


def swap(array, axis):
    return lax.ppermute(array, axis, [(0, 1), (1, 0)])


def ring_start(block, phase):
    return [block, *lax.optimization_barrier((shift(block, phase, 1), shift(block, phase, -1)))]


def ring_up(blocks, phase):
    return [*blocks, shift(blocks[1], phase, 1)]


def ring_both(blocks, phase):
    half = blocks[0].shape[0] // 2
    far = (shift(blocks[1][:half], phase, 1), shift(blocks[2][half:], phase, -1))
    return [*blocks, *lax.optimization_barrier(far)]


def product(grad_rows, act_rows):
    return lax.dot_general(
        grad_rows, act_rows, (((0,), (0,)), ((), ())), preferred_element_type=jnp.float32
    )


def arrange_kernel(place, *refs):
    *sources, out, sems = refs
    tokens = sources[0].shape[0] // 16
    copies = []
    for i in range(16):
        rows = pl.ds(pl.multiple_of(place[i] * tokens, tokens), tokens)
        for source in sources:
            at = pl.ds(len(copies) * tokens, tokens)
            copies.append(
                pltpu.make_async_copy(source.at[rows], out.at[at], sems.at[len(copies)])
            )
    for copy in copies:
        copy.start()
    for copy in copies:
        copy.wait()


def arranged(places, *sources):
    rows, width = sources[0].shape
    rows *= len(sources)
    size = rows * width * 2
    out = pl.pallas_call(
        arrange_kernel,
        in_specs=[pl.BlockSpec(memory_space=pltpu.SMEM)]
        + [pl.BlockSpec(memory_space=pl.ANY)] * len(sources),
        out_specs=pl.BlockSpec(memory_space=pltpu.VMEM),
        out_shape=jax.ShapeDtypeStruct((rows, width), sources[0].dtype),
        scratch_shapes=[pltpu.SemaphoreType.DMA((16 * len(sources),))],
        compiler_params=pltpu.CompilerParams(vmem_limit_bytes=size + (2 << 20)),
        cost_estimate=pl.CostEstimate(flops=0, bytes_accessed=2 * size, transcendentals=0),
    )(places, *sources)
    return out.reshape(4, rows // 4, width)


def total_over(vector, axes):
    spread = jnp.broadcast_to(vector.reshape(1, 8, 128), (16, 8, 128))
    return jnp.sum(lax.all_to_all(spread, axes, 0, 0, tiled=True), axis=0).reshape(1024)


def local(activations, out_grads, weights, momentum, scores, row_moment, col_moment):
    token_scale = 1.0 / math.sqrt(activations.shape[0] * 4)
    core, low = lax.axis_index("core"), lax.axis_index("zl")
    x, y = lax.axis_index("x"), lax.axis_index("y")
    rows = FF // 16

    def units(a, b):
        return lax.dynamic_slice_in_dim(out_grads, ((low ^ a) * 2 + (core ^ b)) * rows, rows, 1)

    other = swap(jnp.concatenate([units(0, 1), units(1, 1)], axis=0), "core")
    tokens = other.shape[0] // 2
    near = jnp.concatenate([units(0, 0), other[:tokens]], axis=0)
    away = swap(jnp.concatenate([units(1, 0), other[tokens:]], axis=0), "zl")
    acts_core = swap(activations, "core")

    places = []
    for j in STEPS:
        for i in STEPS:
            dx, dy = jnp.where(core == 0, i, j), jnp.where(core == 0, j, i)
            places.append((x + dx) % 4 * 4 + (y + dy) % 4)
    places = jnp.stack(places).astype(jnp.int32)

    near = ring_up(ring_start(near, 0), 0)
    near[3], away, acts_core, sent = lax.optimization_barrier(
        (near[3], away, acts_core, activations)
    )
    near = ring_start(jnp.concatenate(near, axis=0), 1)
    away = ring_up(ring_start(away, 0), 0)
    acts_low = swap(sent, "zl")
    first = arranged(places, activations, acts_core)
    *near, away[3] = lax.optimization_barrier((*near, away[3]))
    near = ring_both(near, 1)
    gradient = product(near[0], first[0]) + product(near[1], first[1]) + product(near[2], first[2])
    away = ring_start(jnp.concatenate(away, axis=0), 1)
    near[3], near[4], acts_low = lax.optimization_barrier((near[3], near[4], acts_low))
    second = arranged(places, acts_low, swap(acts_low, "core"))
    *away, near[3], near[4], second, gradient = lax.optimization_barrier(
        (*away, near[3], near[4], second, gradient)
    )
    away = ring_both(away, 1)
    half = near[3].shape[0]
    gradient = gradient + product(near[3], first[3][:half]) + product(near[4], first[3][half:])
    gradient = gradient + product(away[0], second[0])
    gradient = gradient + product(away[1], second[1]) + product(away[2], second[2])
    last = (product(away[3], second[3][:half]), product(away[4], second[3][half:]))
    last = lax.optimization_barrier(last)
    gradient = gradient + (last[0] + last[1])
    gradient = gradient * token_scale

    squares = gradient * gradient + 1e-30
    row_full = total_over(jnp.sum(squares, axis=1), ("x", "y"))
    row_moment_new = 0.8 * row_moment + 0.2 * row_full / D
    col_part = jnp.sum(squares, axis=0)
    sums = jnp.concatenate([col_part, jnp.sum(row_moment_new.reshape(2, 512), axis=0)])
    scores_new = scores - 50.0 * weights * gradient
    sums = total_over(sums, ("zl", "core", "zh"))
    sums, weights, gradient = lax.optimization_barrier((sums, weights, gradient))
    col_moment_new = 0.8 * col_moment + 0.2 * sums[:512] / FF
    row_average = jnp.sum(sums[512:]) / FF
    scale = lax.rsqrt(row_moment_new)[:, None] * lax.rsqrt(col_moment_new / row_average)[None, :]
    momentum_new = (0.9 * momentum.astype(jnp.float32) + 0.1 * (gradient * scale)).astype(jnp.bfloat16)
    weights_new = weights - 0.01 * momentum_new.astype(jnp.float32)
    return (weights_new, momentum_new, scores_new, row_moment_new, col_moment_new)


def solution(mesh):
    fine = Mesh(mesh.devices.reshape(2, 2, 4, 4, 4), ("zl", "core", "x", "y", "zh"))
    dp, row, col = ("zl", "core"), ("x", "y"), "zh"
    return jax.shard_map(
        local,
        mesh=fine,
        in_specs=(
            P(dp, row),
            P(dp + row, col),
            P((col,) + dp, row),
            P((col,) + dp, row),
            P((col,) + dp, row),
            P((col,) + dp),
            P(row),
        ),
        out_specs=(
            P((col,) + dp, row),
            P((col,) + dp, row),
            P((col,) + dp, row),
            P((col,) + dp),
            P(row),
        ),
        check_vma=False,
    )
```

```python
import math

import jax
import jax.numpy as jnp
from jax import lax
from jax.experimental import pallas as pl
from jax.experimental.pallas import tpu as pltpu
from jax.sharding import Mesh, PartitionSpec as P

D = 8192
FF = 16384
AXES = ("core", "x", "y")
STEPS = (0, -1, 1, 2)


def ring_pairs(phase, step):
    pairs = []
    for core in range(2):
        for x in range(4):
            for y in range(4):
                if core == phase:
                    to = (x + step) % 4 * 4 + y
                else:
                    to = x * 4 + (y + step) % 4
                pairs.append((core * 16 + x * 4 + y, core * 16 + to))
    return pairs


def shift(array, phase, step):
    return lax.ppermute(array, AXES, ring_pairs(phase, step))


def along_z(array, step):
    place = lambda z: z % 2 * 4 + z // 2
    return lax.ppermute(array, ("zl", "zh"), [(place(z), place((z + step) % 8)) for z in range(8)])


def swap(array, axis):
    return lax.ppermute(array, axis, [(0, 1), (1, 0)])


def ring_start(block, phase):
    pair = (shift(block, phase, 1), shift(block, phase, -1))
    return [block, *(pair if phase else lax.optimization_barrier(pair))]


def ring_end(blocks, phase, step):
    return [*blocks, shift(blocks[1] if step == 1 else blocks[2], phase, step)]


def after(blocks, *others):
    return lax.optimization_barrier((*blocks, *others))[: len(blocks)]


def product(grad_rows, act_rows):
    return lax.dot_general(
        grad_rows, act_rows, (((0,), (0,)), ((), ())), preferred_element_type=jnp.float32
    )


def arrange_kernel(place, first, second, out, sems):
    tokens = first.shape[0] // 16
    copies = []
    for i in range(16):
        rows = pl.ds(pl.multiple_of(place[i] * tokens, tokens), tokens)
        for c, source in enumerate((first, second)):
            at = pl.ds((2 * i + c) * tokens, tokens)
            copies.append(pltpu.make_async_copy(source.at[rows], out.at[at], sems.at[2 * i + c]))
    for copy in copies:
        copy.start()
    for copy in copies:
        copy.wait()


def arranged(places, first, second):
    rows, width = first.shape
    anywhere = pl.BlockSpec(memory_space=pl.ANY)
    out = pl.pallas_call(
        arrange_kernel,
        in_specs=[pl.BlockSpec(memory_space=pltpu.SMEM), anywhere, anywhere],
        out_specs=pl.BlockSpec(memory_space=pltpu.VMEM),
        out_shape=jax.ShapeDtypeStruct((2 * rows, width), first.dtype),
        scratch_shapes=[pltpu.SemaphoreType.DMA((32,))],
        compiler_params=pltpu.CompilerParams(vmem_limit_bytes=8 << 20),
        cost_estimate=pl.CostEstimate(
            flops=0, bytes_accessed=8 * rows * width, transcendentals=0
        ),
    )(places, first, second)
    return out.reshape(4, rows // 2, width)


def total_over(vector, axes):
    spread = jnp.broadcast_to(vector[None], (16, vector.shape[0]))
    return jnp.sum(lax.all_to_all(spread, axes, 0, 0, tiled=True), axis=0)


def local(activations, out_grads, weights, momentum, scores, row_moment, col_moment):
    token_scale = 1.0 / math.sqrt(activations.shape[0] * 4)
    core, low = lax.axis_index("core"), lax.axis_index("zl")
    x, y = lax.axis_index("x"), lax.axis_index("y")
    rows = FF // 16

    def units(a, b):
        return lax.dynamic_slice_in_dim(out_grads, ((low ^ a) * 2 + (core ^ b)) * rows, rows, 1)

    other = swap(jnp.concatenate([units(0, 1), units(1, 1)], axis=0), "core")
    tokens = other.shape[0] // 2
    near = jnp.concatenate([units(0, 0), other[:tokens]], axis=0)
    away = swap(jnp.concatenate([units(1, 0), other[tokens:]], axis=0), "zl")
    acts_core = swap(activations, "core")

    places = []
    for j in STEPS:
        for i in STEPS:
            dx, dy = jnp.where(core == 0, i, j), jnp.where(core == 0, j, i)
            places.append((x + dx) % 4 * 4 + (y + dy) % 4)
    places = jnp.stack(places).astype(jnp.int32)

    near = ring_end(ring_start(near, 0), 0, 1)
    near[3], away, acts_core, sent = lax.optimization_barrier(
        (near[3], away, acts_core, activations)
    )
    near = ring_start(jnp.concatenate(near, axis=0), 1)
    near[1], near[2] = lax.optimization_barrier((near[1], near[2]))
    away = ring_end(ring_start(away, 0), 0, -1)
    half = sent.shape[0] // 2
    acts_low = (along_z(sent[:half], 1), along_z(sent[half:], -1))
    first = arranged(places, activations, acts_core)
    gradient = product(near[0], first[0]) + product(near[1], first[1]) + product(near[2], first[2])
    near = ring_end(after(near, *away), 1, 1)
    away = ring_start(jnp.concatenate(away, axis=0), 1)
    away[2], gradient = lax.optimization_barrier((away[2], gradient))
    away = ring_end(away, 1, -1)
    acts_low = jnp.concatenate(after(acts_low, away[2]), axis=0)
    second = arranged(places, acts_low, swap(acts_low, "core"))
    gradient = gradient + product(near[3], first[3])
    gradient = gradient + product(away[0], second[0]) + product(away[2], second[2])
    last = lax.optimization_barrier((product(away[1], second[1]), product(away[3], second[3])))
    gradient = gradient + (last[0] + last[1])
    gradient = gradient * token_scale

    squares = gradient * gradient + 1e-30
    row_full = total_over(jnp.sum(squares, axis=1), ("x", "y"))
    row_moment_new = 0.8 * row_moment + 0.2 * row_full / D
    col_part = jnp.sum(squares, axis=0)
    sums = jnp.concatenate([col_part, jnp.sum(row_moment_new.reshape(8, 128), axis=0)])
    scores_new = scores - 50.0 * weights * gradient
    sums = total_over(sums, ("zl", "core", "zh"))
    sums, weights, gradient = lax.optimization_barrier((sums, weights, gradient))
    col_moment_new = 0.8 * col_moment + 0.2 * sums[:512] / FF
    row_average = jnp.sum(sums[512:]) / FF
    scale = lax.rsqrt(row_moment_new)[:, None] * lax.rsqrt(col_moment_new / row_average)[None, :]
    momentum_new = (0.9 * momentum.astype(jnp.float32) + 0.1 * (gradient * scale)).astype(jnp.bfloat16)
    weights_new = weights - 0.01 * momentum_new.astype(jnp.float32)
    return (weights_new, momentum_new, scores_new, row_moment_new, col_moment_new)


def solution(mesh):
    fine = Mesh(mesh.devices.reshape(2, 2, 4, 4, 4), ("zl", "core", "x", "y", "zh"))
    dp, row, col = ("zl", "core"), ("x", "y"), "zh"
    return jax.shard_map(
        local,
        mesh=fine,
        in_specs=(
            P(dp, row),
            P(dp + row, col),
            P((col,) + dp, row),
            P((col,) + dp, row),
            P((col,) + dp, row),
            P((col,) + dp),
            P(row),
        ),
        out_specs=(
            P((col,) + dp, row),
            P((col,) + dp, row),
            P((col,) + dp, row),
            P((col,) + dp),
            P(row),
        ),
        check_vma=False,
    )
```

```python
import math

import jax
import jax.numpy as jnp
from jax import lax
from jax.experimental import pallas as pl
from jax.experimental.pallas import tpu as pltpu
from jax.sharding import Mesh, PartitionSpec as P

D = 8192
FF = 16384
AXES = ("core", "x", "y")
STEPS = (0, -1, 1, 2)


def ring_pairs(phase, step):
    pairs = []
    for core in range(2):
        for x in range(4):
            for y in range(4):
                if core == phase:
                    to = (x + step) % 4 * 4 + y
                else:
                    to = x * 4 + (y + step) % 4
                pairs.append((core * 16 + x * 4 + y, core * 16 + to))
    return pairs


def shift(array, phase, step):
    return lax.ppermute(array, AXES, ring_pairs(phase, step))


def along_z(array, step):
    place = lambda z: z % 2 * 4 + z // 2
    return lax.ppermute(array, ("zl", "zh"), [(place(z), place((z + step) % 8)) for z in range(8)])


def swap(array, axis):
    return lax.ppermute(array, axis, [(0, 1), (1, 0)])


def ring_start(block, phase):
    return [block, shift(block, phase, 1), shift(block, phase, -1)]


def ring_end(blocks, phase, step):
    return [*blocks, shift(blocks[1] if step == 1 else blocks[2], phase, step)]


def after(blocks, *others):
    return lax.optimization_barrier((*blocks, *others))[: len(blocks)]


def product(grad_rows, act_rows):
    return lax.dot_general(
        grad_rows, act_rows, (((0,), (0,)), ((), ())), preferred_element_type=jnp.float32
    )


def arrange_kernel(place, first, second, out, sems):
    tokens = first.shape[0] // 16
    copies = []
    for i in range(16):
        rows = pl.ds(pl.multiple_of(place[i] * tokens, tokens), tokens)
        for c, source in enumerate((first, second)):
            at = pl.ds((2 * i + c) * tokens, tokens)
            copies.append(pltpu.make_async_copy(source.at[rows], out.at[at], sems.at[2 * i + c]))
    for copy in copies:
        copy.start()
    for copy in copies:
        copy.wait()


def arranged(places, first, second):
    rows, width = first.shape
    anywhere = pl.BlockSpec(memory_space=pl.ANY)
    out = pl.pallas_call(
        arrange_kernel,
        in_specs=[pl.BlockSpec(memory_space=pltpu.SMEM), anywhere, anywhere],
        out_specs=pl.BlockSpec(memory_space=pltpu.VMEM),
        out_shape=jax.ShapeDtypeStruct((2 * rows, width), first.dtype),
        scratch_shapes=[pltpu.SemaphoreType.DMA((32,))],
        compiler_params=pltpu.CompilerParams(vmem_limit_bytes=8 << 20),
        cost_estimate=pl.CostEstimate(
            flops=0, bytes_accessed=8 * rows * width, transcendentals=0
        ),
    )(places, first, second)
    return out.reshape(4, rows // 2, width)


def total_over(vector, axes):
    spread = jnp.broadcast_to(vector[None], (16, vector.shape[0]))
    return jnp.sum(lax.all_to_all(spread, axes, 0, 0, tiled=True), axis=0)


def local(activations, out_grads, weights, momentum, scores, row_moment, col_moment):
    token_scale = 1.0 / math.sqrt(activations.shape[0] * 4)
    core, low = lax.axis_index("core"), lax.axis_index("zl")
    x, y = lax.axis_index("x"), lax.axis_index("y")
    rows = FF // 16

    def units(a, b):
        return lax.dynamic_slice_in_dim(out_grads, ((low ^ a) * 2 + (core ^ b)) * rows, rows, 1)

    other = swap(jnp.concatenate([units(0, 1), units(1, 1)], axis=0), "core")
    tokens = other.shape[0] // 2
    near = jnp.concatenate([units(0, 0), other[:tokens]], axis=0)
    away = swap(jnp.concatenate([units(1, 0), other[tokens:]], axis=0), "zl")
    acts_core = swap(activations, "core")

    places = []
    for j in STEPS:
        for i in STEPS:
            dx, dy = jnp.where(core == 0, i, j), jnp.where(core == 0, j, i)
            places.append((x + dx) % 4 * 4 + (y + dy) % 4)
    places = jnp.stack(places).astype(jnp.int32)

    near = ring_end(ring_start(near, 0), 0, 1)
    near[3:] = after(near[3:], away)
    (sent,) = after((activations,), *near)
    near = ring_start(jnp.concatenate(near, axis=0), 1)
    away = ring_end(ring_start(away, 0), 0, -1)
    half = sent.shape[0] // 2
    acts_low = (along_z(sent[:half], 1), along_z(sent[half:], -1))
    first = arranged(places, activations, acts_core)
    gradient = product(near[0], first[0]) + product(near[1], first[1]) + product(near[2], first[2])
    near = ring_end(after(near, *away), 1, 1)
    away = ring_start(jnp.concatenate(away, axis=0), 1)
    away[2], gradient = lax.optimization_barrier((away[2], gradient))
    away = ring_end(away, 1, -1)
    acts_low = jnp.concatenate(after(acts_low, away[2]), axis=0)
    second = arranged(places, acts_low, swap(acts_low, "core"))
    gradient = gradient + product(near[3], first[3])
    gradient = gradient + product(away[0], second[0]) + product(away[2], second[2])
    last = lax.optimization_barrier((product(away[1], second[1]), product(away[3], second[3])))
    gradient = gradient + (last[0] + last[1])
    gradient = gradient * token_scale

    squares = gradient * gradient + 1e-30
    row_full = total_over(jnp.sum(squares, axis=1), ("x", "y"))
    row_moment_new = 0.8 * row_moment + 0.2 * row_full / D
    col_part = jnp.sum(squares, axis=0)
    sums = jnp.concatenate([col_part, jnp.sum(row_moment_new.reshape(8, 128), axis=0)])
    sums = total_over(sums, ("zl", "core", "zh"))
    col_moment_new = 0.8 * col_moment + 0.2 * sums[:512] / FF
    row_average = jnp.sum(sums[512:]) / FF
    row_scale, col_scale = lax.rsqrt(row_moment_new), lax.rsqrt(col_moment_new / row_average)
    update = gradient * (row_scale[:, None] * col_scale[None, :])
    momentum_new = (0.9 * momentum.astype(jnp.float32) + 0.1 * update).astype(jnp.bfloat16)
    weights_new = weights - 0.01 * momentum_new.astype(jnp.float32)
    scores_new = scores - 50.0 * weights * gradient
    return (weights_new, momentum_new, scores_new, row_moment_new, col_moment_new)


def solution(mesh):
    fine = Mesh(mesh.devices.reshape(2, 2, 4, 4, 4), ("zl", "core", "x", "y", "zh"))
    dp, row, col = ("zl", "core"), ("x", "y"), "zh"
    return jax.shard_map(
        local,
        mesh=fine,
        in_specs=(
            P(dp, row),
            P(dp + row, col),
            P((col,) + dp, row),
            P((col,) + dp, row),
            P((col,) + dp, row),
            P((col,) + dp),
            P(row),
        ),
        out_specs=(
            P((col,) + dp, row),
            P((col,) + dp, row),
            P((col,) + dp, row),
            P((col,) + dp),
            P(row),
        ),
        check_vma=False,
    )
```

```python
import math

import jax
import jax.numpy as jnp
from jax import lax
from jax.experimental import pallas as pl
from jax.experimental.pallas import tpu as pltpu
from jax.sharding import Mesh, PartitionSpec as P

D = 8192
FF = 16384
AXES = ("core", "x", "y")
STEPS = (0, -1, 1, 2)


def ring_pairs(phase, step):
    pairs = []
    for core in range(2):
        for x in range(4):
            for y in range(4):
                if core == phase:
                    to = (x + step) % 4 * 4 + y
                else:
                    to = x * 4 + (y + step) % 4
                pairs.append((core * 16 + x * 4 + y, core * 16 + to))
    return pairs


def shift(array, phase, step):
    return lax.ppermute(array, AXES, ring_pairs(phase, step))


def along_z(array, step):
    place = lambda z: z % 2 * 4 + z // 2
    return lax.ppermute(array, ("zl", "zh"), [(place(z), place((z + step) % 8)) for z in range(8)])


def swap(array, axis):
    return lax.ppermute(array, axis, [(0, 1), (1, 0)])


def ring_start(block, phase):
    return [block, shift(block, phase, 1), shift(block, phase, -1)]


def ring_end(blocks, phase, step):
    return [*blocks, shift(blocks[1] if step == 1 else blocks[2], phase, step)]


def after(blocks, *others):
    return lax.optimization_barrier((*blocks, *others))[: len(blocks)]


def product(grad_rows, act_rows):
    return lax.dot_general(
        grad_rows, act_rows, (((0,), (0,)), ((), ())), preferred_element_type=jnp.float32
    )


def arrange_kernel(place, first, second, out, sems):
    tokens = first.shape[0] // 16
    copies = []
    for i in range(16):
        rows = pl.ds(pl.multiple_of(place[i] * tokens, tokens), tokens)
        for c, source in enumerate((first, second)):
            at = pl.ds((2 * i + c) * tokens, tokens)
            copies.append(pltpu.make_async_copy(source.at[rows], out.at[at], sems.at[2 * i + c]))
    for copy in copies:
        copy.start()
    for copy in copies:
        copy.wait()


def arranged(places, first, second):
    rows, width = first.shape
    anywhere = pl.BlockSpec(memory_space=pl.ANY)
    out = pl.pallas_call(
        arrange_kernel,
        in_specs=[pl.BlockSpec(memory_space=pltpu.SMEM), anywhere, anywhere],
        out_specs=pl.BlockSpec(memory_space=pltpu.VMEM),
        out_shape=jax.ShapeDtypeStruct((2 * rows, width), first.dtype),
        scratch_shapes=[pltpu.SemaphoreType.DMA((32,))],
        compiler_params=pltpu.CompilerParams(vmem_limit_bytes=8 << 20),
        cost_estimate=pl.CostEstimate(
            flops=0, bytes_accessed=8 * rows * width, transcendentals=0
        ),
    )(places, first, second)
    return out.reshape(4, rows // 2, width)


def total_over(vector, axes):
    spread = jnp.broadcast_to(vector[None], (16, vector.shape[0]))
    return jnp.sum(lax.all_to_all(spread, axes, 0, 0, tiled=True), axis=0)


def local(activations, out_grads, weights, momentum, scores, row_moment, col_moment):
    token_scale = 1.0 / math.sqrt(activations.shape[0] * 4)
    core, low = lax.axis_index("core"), lax.axis_index("zl")
    x, y = lax.axis_index("x"), lax.axis_index("y")
    rows = FF // 16

    def units(a, b):
        return lax.dynamic_slice_in_dim(out_grads, ((low ^ a) * 2 + (core ^ b)) * rows, rows, 1)

    other = swap(jnp.concatenate([units(0, 1), units(1, 1)], axis=0), "core")
    tokens = other.shape[0] // 2
    near = jnp.concatenate([units(0, 0), other[:tokens]], axis=0)
    away = swap(jnp.concatenate([units(1, 0), other[tokens:]], axis=0), "zl")
    acts_core = swap(activations, "core")

    places = []
    for j in STEPS:
        for i in STEPS:
            dx, dy = jnp.where(core == 0, i, j), jnp.where(core == 0, j, i)
            places.append((x + dx) % 4 * 4 + (y + dy) % 4)
    places = jnp.stack(places).astype(jnp.int32)

    near = [*ring_start(near, 0), shift(near, 0, 2)]
    near[3:] = after(near[3:], away)
    (sent,) = after((activations,), *near)
    near = ring_start(jnp.concatenate(near, axis=0), 1)
    away = ring_end(ring_start(away, 0), 0, -1)
    half = sent.shape[0] // 2
    acts_low = (along_z(sent[:half], 1), along_z(sent[half:], -1))
    first = arranged(places, activations, acts_core)
    gradient = product(near[0], first[0]) + product(near[1], first[1]) + product(near[2], first[2])
    near = ring_end(after(near, *away), 1, 1)
    away = ring_start(jnp.concatenate(away, axis=0), 1)
    away[2], gradient = lax.optimization_barrier((away[2], gradient))
    away = ring_end(away, 1, -1)
    acts_low = jnp.concatenate(after(acts_low, away[2]), axis=0)
    second = arranged(places, acts_low, swap(acts_low, "core"))
    gradient = gradient + product(near[3], first[3])
    gradient = gradient + product(away[0], second[0]) + product(away[2], second[2])
    last = lax.optimization_barrier((product(away[1], second[1]), product(away[3], second[3])))
    gradient = gradient + (last[0] + last[1])
    gradient = gradient * token_scale

    squares = gradient * gradient + 1e-30
    row_full = total_over(jnp.sum(squares, axis=1), ("x", "y"))
    row_moment_new = 0.8 * row_moment + 0.2 * row_full / D
    col_part = jnp.sum(squares, axis=0)
    sums = jnp.concatenate([col_part, jnp.sum(row_moment_new.reshape(8, 128), axis=0)])
    scores_new = scores - 50.0 * weights * gradient
    sums = total_over(sums, ("zl", "core", "zh"))
    sums, weights, gradient = lax.optimization_barrier((sums, weights, gradient))
    col_moment_new = 0.8 * col_moment + 0.2 * sums[:512] / FF
    row_average = jnp.sum(sums[512:]) / FF
    scale = lax.rsqrt(row_moment_new)[:, None] * lax.rsqrt(col_moment_new / row_average)[None, :]
    momentum_new = (0.9 * momentum.astype(jnp.float32) + 0.1 * (gradient * scale)).astype(jnp.bfloat16)
    weights_new = weights - 0.01 * momentum_new.astype(jnp.float32)
    return (weights_new, momentum_new, scores_new, row_moment_new, col_moment_new)


def solution(mesh):
    fine = Mesh(mesh.devices.reshape(2, 2, 4, 4, 4), ("zl", "core", "x", "y", "zh"))
    dp, row, col = ("zl", "core"), ("x", "y"), "zh"
    return jax.shard_map(
        local,
        mesh=fine,
        in_specs=(
            P(dp, row),
            P(dp + row, col),
            P((col,) + dp, row),
            P((col,) + dp, row),
            P((col,) + dp, row),
            P((col,) + dp),
            P(row),
        ),
        out_specs=(
            P((col,) + dp, row),
            P((col,) + dp, row),
            P((col,) + dp, row),
            P((col,) + dp),
            P(row),
        ),
        check_vma=False,
    )
```

```python
import math

import jax
import jax.numpy as jnp
from jax import lax
from jax.experimental import pallas as pl
from jax.experimental.pallas import tpu as pltpu
from jax.sharding import Mesh, PartitionSpec as P

D = 8192
FF = 16384
AXES = ("core", "x", "y")
STEPS = (0, -1, 1, 2)


def ring_pairs(phase, step):
    pairs = []
    for core in range(2):
        for x in range(4):
            for y in range(4):
                if core == phase:
                    to = (x + step) % 4 * 4 + y
                else:
                    to = x * 4 + (y + step) % 4
                pairs.append((core * 16 + x * 4 + y, core * 16 + to))
    return pairs


def shift(array, phase, step):
    return lax.ppermute(array, AXES, ring_pairs(phase, step))


def along_z(array, step):
    place = lambda z: z % 2 * 4 + z // 2
    return lax.ppermute(array, ("zl", "zh"), [(place(z), place((z + step) % 8)) for z in range(8)])


def swap(array, axis):
    return lax.ppermute(array, axis, [(0, 1), (1, 0)])


def ring_start(block, phase):
    return [block, shift(block, phase, 1), shift(block, phase, -1)]


def ring_end(blocks, phase, step):
    return [*blocks, shift(blocks[1] if step == 1 else blocks[2], phase, step)]


def after(blocks, *others):
    return lax.optimization_barrier((*blocks, *others))[: len(blocks)]


def product(grad_rows, act_rows):
    return lax.dot_general(
        grad_rows, act_rows, (((0,), (0,)), ((), ())), preferred_element_type=jnp.float32
    )


def arrange_kernel(place, first, second, out, sems):
    tokens = first.shape[0] // 16
    copies = []
    for i in range(16):
        rows = pl.ds(pl.multiple_of(place[i] * tokens, tokens), tokens)
        for c, source in enumerate((first, second)):
            at = pl.ds((2 * i + c) * tokens, tokens)
            copies.append(pltpu.make_async_copy(source.at[rows], out.at[at], sems.at[2 * i + c]))
    for copy in copies:
        copy.start()
    for copy in copies:
        copy.wait()


def arranged(places, first, second):
    rows, width = first.shape
    anywhere = pl.BlockSpec(memory_space=pl.ANY)
    out = pl.pallas_call(
        arrange_kernel,
        in_specs=[pl.BlockSpec(memory_space=pltpu.SMEM), anywhere, anywhere],
        out_specs=pl.BlockSpec(memory_space=pltpu.VMEM),
        out_shape=jax.ShapeDtypeStruct((2 * rows, width), first.dtype),
        scratch_shapes=[pltpu.SemaphoreType.DMA((32,))],
        compiler_params=pltpu.CompilerParams(vmem_limit_bytes=8 << 20),
        cost_estimate=pl.CostEstimate(
            flops=0, bytes_accessed=8 * rows * width, transcendentals=0
        ),
    )(places, first, second)
    return out.reshape(4, rows // 2, width)


def total_over(vector, axes):
    spread = jnp.broadcast_to(vector[None], (16, vector.shape[0]))
    return jnp.sum(lax.all_to_all(spread, axes, 0, 0, tiled=True), axis=0)


def local(activations, out_grads, weights, momentum, scores, row_moment, col_moment):
    token_scale = 1.0 / math.sqrt(activations.shape[0] * 4)
    core, low = lax.axis_index("core"), lax.axis_index("zl")
    x, y = lax.axis_index("x"), lax.axis_index("y")
    rows = FF // 16

    def units(a, b):
        return lax.dynamic_slice_in_dim(out_grads, ((low ^ a) * 2 + (core ^ b)) * rows, rows, 1)

    low_blocks = swap(jnp.concatenate([units(1, 0), units(1, 1)], axis=0), "zl")
    near = units(0, 0)
    tokens = near.shape[0]
    near = jnp.concatenate([near, swap(units(0, 1), "core")], axis=0)
    away = jnp.concatenate([low_blocks[:tokens], swap(low_blocks[tokens:], "core")], axis=0)
    acts_core = swap(activations, "core")

    places = []
    for j in STEPS:
        for i in STEPS:
            dx, dy = jnp.where(core == 0, i, j), jnp.where(core == 0, j, i)
            places.append((x + dx) % 4 * 4 + (y + dy) % 4)
    places = jnp.stack(places).astype(jnp.int32)

    near = [*ring_start(near, 0), shift(near, 0, 2)]
    near[3:] = after(near[3:], away)
    (sent,) = after((activations,), *near)
    near = ring_start(jnp.concatenate(near, axis=0), 1)
    away = ring_end(ring_start(away, 0), 0, -1)
    half = sent.shape[0] // 2
    acts_low = (along_z(sent[:half], 1), along_z(sent[half:], -1))
    first = arranged(places, activations, acts_core)
    gradient = product(near[0], first[0]) + product(near[1], first[1]) + product(near[2], first[2])
    near = ring_end(after(near, *away), 1, 1)
    away = ring_start(jnp.concatenate(away, axis=0), 1)
    away[2], gradient = lax.optimization_barrier((away[2], gradient))
    away = ring_end(away, 1, -1)
    acts_low = jnp.concatenate(after(acts_low, away[2]), axis=0)
    second = arranged(places, acts_low, swap(acts_low, "core"))
    gradient = gradient + product(near[3], first[3])
    gradient = gradient + product(away[0], second[0]) + product(away[2], second[2])
    last = lax.optimization_barrier((product(away[1], second[1]), product(away[3], second[3])))
    gradient = gradient + (last[0] + last[1])
    gradient = gradient * token_scale

    squares = gradient * gradient + 1e-30
    row_part, col_part = jnp.sum(squares, axis=1), jnp.sum(squares, axis=0)
    row_part, gradient = lax.optimization_barrier((row_part, gradient))
    scores_new = scores - 50.0 * weights * gradient
    row_full = total_over(row_part, ("x", "y"))
    row_moment_new = 0.8 * row_moment + 0.2 * row_full / D
    sums = jnp.concatenate([col_part, jnp.sum(row_moment_new.reshape(8, 128), axis=0)])
    sums = total_over(sums, ("zl", "core", "zh"))
    sums, scores_new, weights, gradient = lax.optimization_barrier(
        (sums, scores_new, weights, gradient)
    )
    col_moment_new = 0.8 * col_moment + 0.2 * sums[:512] / FF
    row_average = jnp.sum(sums[512:]) / FF
    row_scale, col_scale = lax.rsqrt(row_moment_new), lax.rsqrt(col_moment_new / row_average)
    update = gradient * (row_scale[:, None] * col_scale[None, :])
    momentum_new = (0.9 * momentum.astype(jnp.float32) + 0.1 * update).astype(jnp.bfloat16)
    weights_new = weights - 0.01 * momentum_new.astype(jnp.float32)
    return (weights_new, momentum_new, scores_new, row_moment_new, col_moment_new)


def solution(mesh):
    fine = Mesh(mesh.devices.reshape(2, 2, 4, 4, 4), ("zl", "core", "x", "y", "zh"))
    dp, row, col = ("zl", "core"), ("x", "y"), "zh"
    return jax.shard_map(
        local,
        mesh=fine,
        in_specs=(
            P(dp, row),
            P(dp + row, col),
            P((col,) + dp, row),
            P((col,) + dp, row),
            P((col,) + dp, row),
            P((col,) + dp),
            P(row),
        ),
        out_specs=(
            P((col,) + dp, row),
            P((col,) + dp, row),
            P((col,) + dp, row),
            P((col,) + dp),
            P(row),
        ),
        check_vma=False,
    )
```

```python
import math

import jax
import jax.numpy as jnp
from jax import lax
from jax.experimental import pallas as pl
from jax.experimental.pallas import tpu as pltpu
from jax.sharding import Mesh, PartitionSpec as P

D = 8192
FF = 16384
AXES = ("core", "x", "y")
STEPS = (0, -1, 1, 2)


def ring_pairs(phase, step):
    pairs = []
    for core in range(2):
        for x in range(4):
            for y in range(4):
                if core == phase:
                    to = (x + step) % 4 * 4 + y
                else:
                    to = x * 4 + (y + step) % 4
                pairs.append((core * 16 + x * 4 + y, core * 16 + to))
    return pairs


def shift(array, phase, step):
    return lax.ppermute(array, AXES, ring_pairs(phase, step))


def along_z(array, step):
    place = lambda z: z % 2 * 4 + z // 2
    return lax.ppermute(array, ("zl", "zh"), [(place(z), place((z + step) % 8)) for z in range(8)])


def swap(array, axis):
    return lax.ppermute(array, axis, [(0, 1), (1, 0)])


def ring_start(block, phase):
    return [block, shift(block, phase, 1), shift(block, phase, -1)]


def ring_end(blocks, phase, step):
    return [*blocks, shift(blocks[1] if step == 1 else blocks[2], phase, step)]


def after(blocks, *others):
    return lax.optimization_barrier((*blocks, *others))[: len(blocks)]


def product(grad_rows, act_rows):
    return lax.dot_general(
        grad_rows, act_rows, (((0,), (0,)), ((), ())), preferred_element_type=jnp.float32
    )


def arrange_kernel(place, first, second, out, sems):
    tokens = first.shape[0] // 16
    copies = []
    for i in range(16):
        rows = pl.ds(pl.multiple_of(place[i] * tokens, tokens), tokens)
        for c, source in enumerate((first, second)):
            at = pl.ds((2 * i + c) * tokens, tokens)
            copies.append(pltpu.make_async_copy(source.at[rows], out.at[at], sems.at[2 * i + c]))
    for copy in copies:
        copy.start()
    for copy in copies:
        copy.wait()


def arranged(places, first, second):
    rows, width = first.shape
    anywhere = pl.BlockSpec(memory_space=pl.ANY)
    out = pl.pallas_call(
        arrange_kernel,
        in_specs=[pl.BlockSpec(memory_space=pltpu.SMEM), anywhere, anywhere],
        out_specs=pl.BlockSpec(memory_space=pltpu.VMEM),
        out_shape=jax.ShapeDtypeStruct((2 * rows, width), first.dtype),
        scratch_shapes=[pltpu.SemaphoreType.DMA((32,))],
        compiler_params=pltpu.CompilerParams(vmem_limit_bytes=8 << 20),
        cost_estimate=pl.CostEstimate(
            flops=0, bytes_accessed=8 * rows * width, transcendentals=0
        ),
    )(places, first, second)
    return out.reshape(4, rows // 2, width)


def total_over(vector, axes):
    spread = jnp.broadcast_to(vector[None], (16, vector.shape[0]))
    return jnp.sum(lax.all_to_all(spread, axes, 0, 0, tiled=True), axis=0)


def local(activations, out_grads, weights, momentum, scores, row_moment, col_moment):
    token_scale = 1.0 / math.sqrt(activations.shape[0] * 4)
    core, low = lax.axis_index("core"), lax.axis_index("zl")
    x, y = lax.axis_index("x"), lax.axis_index("y")
    rows = FF // 16

    def units(a, b):
        return lax.dynamic_slice_in_dim(out_grads, ((low ^ a) * 2 + (core ^ b)) * rows, rows, 1)

    low_blocks = swap(jnp.concatenate([units(1, 0), units(1, 1)], axis=0), "zl")
    near = units(0, 0)
    tokens = near.shape[0]
    near = jnp.concatenate([near, swap(units(0, 1), "core")], axis=0)
    away = jnp.concatenate([low_blocks[:tokens], swap(low_blocks[tokens:], "core")], axis=0)
    acts_core = swap(activations, "core")

    places = []
    for j in STEPS:
        for i in STEPS:
            dx, dy = jnp.where(core == 0, i, j), jnp.where(core == 0, j, i)
            places.append((x + dx) % 4 * 4 + (y + dy) % 4)
    places = jnp.stack(places).astype(jnp.int32)

    near = [*ring_start(near, 0), shift(near, 0, 2)]
    near[3:] = after(near[3:], away)
    near = ring_start(jnp.concatenate(near, axis=0), 1)
    away = ring_end(ring_start(away, 0), 0, -1)
    near = list(after(near, *away))
    (sent,) = after((activations,), *near)
    half = sent.shape[0] // 2
    acts_low = (along_z(sent[:half], 1), along_z(sent[half:], -1))
    first = arranged(places, activations, acts_core)
    gradient = product(near[0], first[0]) + product(near[1], first[1]) + product(near[2], first[2])
    away = ring_start(jnp.concatenate(away, axis=0), 1)
    near[1], away[1] = lax.optimization_barrier((near[1], away[1]))
    near = ring_end(near, 1, 1)
    away[2], gradient = lax.optimization_barrier((away[2], gradient))
    away = ring_end(away, 1, -1)
    acts_low = jnp.concatenate(after(acts_low, away[2]), axis=0)
    second = arranged(places, acts_low, swap(acts_low, "core"))
    gradient = gradient + product(away[0], second[0])
    gradient = gradient + product(away[1], second[1]) + product(away[2], second[2])
    gradient = gradient + product(near[3], first[3])
    away[3], gradient = lax.optimization_barrier((away[3], gradient))
    gradient = gradient + lax.optimization_barrier(product(away[3], second[3]))
    gradient = gradient * token_scale

    squares = gradient * gradient + 1e-30
    row_part, col_part = jnp.sum(squares, axis=1), jnp.sum(squares, axis=0)
    row_part, gradient = lax.optimization_barrier((row_part, gradient))
    scores_new = scores - 50.0 * weights * gradient
    row_full = total_over(row_part, ("x", "y"))
    row_moment_new = 0.8 * row_moment + 0.2 * row_full / D
    sums = jnp.concatenate([col_part, jnp.sum(row_moment_new.reshape(8, 128), axis=0)])
    sums = total_over(sums, ("zl", "core", "zh"))
    sums, scores_new, weights, gradient = lax.optimization_barrier(
        (sums, scores_new, weights, gradient)
    )
    col_moment_new = 0.8 * col_moment + 0.2 * sums[:512] / FF
    row_average = jnp.sum(sums[512:]) / FF
    row_scale, col_scale = lax.rsqrt(row_moment_new), lax.rsqrt(col_moment_new / row_average)
    update = gradient * (row_scale[:, None] * col_scale[None, :])
    momentum_new = (0.9 * momentum.astype(jnp.float32) + 0.1 * update).astype(jnp.bfloat16)
    weights_new = weights - 0.01 * momentum_new.astype(jnp.float32)
    return (weights_new, momentum_new, scores_new, row_moment_new, col_moment_new)


def solution(mesh):
    fine = Mesh(mesh.devices.reshape(2, 2, 4, 4, 4), ("zl", "core", "x", "y", "zh"))
    dp, row, col = ("zl", "core"), ("x", "y"), "zh"
    return jax.shard_map(
        local,
        mesh=fine,
        in_specs=(
            P(dp, row),
            P(dp + row, col),
            P((col,) + dp, row),
            P((col,) + dp, row),
            P((col,) + dp, row),
            P((col,) + dp),
            P(row),
        ),
        out_specs=(
            P((col,) + dp, row),
            P((col,) + dp, row),
            P((col,) + dp, row),
            P((col,) + dp),
            P(row),
        ),
        check_vma=False,
    )
```

```python
import math

import jax
import jax.numpy as jnp
from jax import lax
from jax.experimental import pallas as pl
from jax.experimental.pallas import tpu as pltpu
from jax.sharding import Mesh, PartitionSpec as P

D = 8192
FF = 16384
AXES = ("core", "x", "y")
STEPS = (0, -1, 1, 2)


def ring_pairs(phase, step):
    pairs = []
    for core in range(2):
        for x in range(4):
            for y in range(4):
                if core == phase:
                    to = (x + step) % 4 * 4 + y
                else:
                    to = x * 4 + (y + step) % 4
                pairs.append((core * 16 + x * 4 + y, core * 16 + to))
    return pairs


def shift(array, phase, step):
    return lax.ppermute(array, AXES, ring_pairs(phase, step))


def along_z(array, step):
    place = lambda z: z % 2 * 4 + z // 2
    return lax.ppermute(array, ("zl", "zh"), [(place(z), place((z + step) % 8)) for z in range(8)])


def swap(array, axis):
    return lax.ppermute(array, axis, [(0, 1), (1, 0)])


def ring_start(block, phase):
    return [block, shift(block, phase, 1), shift(block, phase, -1)]


def ring_end(blocks, phase, step):
    return [*blocks, shift(blocks[1] if step == 1 else blocks[2], phase, step)]


def after(blocks, *others):
    return lax.optimization_barrier((*blocks, *others))[: len(blocks)]


def product(grad_rows, act_rows):
    return lax.dot_general(
        grad_rows, act_rows, (((0,), (0,)), ((), ())), preferred_element_type=jnp.float32
    )


def arrange_kernel(place, first, second, out, sems):
    tokens = first.shape[0] // 16
    copies = []
    for i in range(16):
        rows = pl.ds(pl.multiple_of(place[i] * tokens, tokens), tokens)
        for c, source in enumerate((first, second)):
            at = pl.ds((2 * i + c) * tokens, tokens)
            copies.append(pltpu.make_async_copy(source.at[rows], out.at[at], sems.at[2 * i + c]))
    for copy in copies:
        copy.start()
    for copy in copies:
        copy.wait()


def arranged(places, first, second):
    rows, width = first.shape
    anywhere = pl.BlockSpec(memory_space=pl.ANY)
    out = pl.pallas_call(
        arrange_kernel,
        in_specs=[pl.BlockSpec(memory_space=pltpu.SMEM), anywhere, anywhere],
        out_specs=pl.BlockSpec(memory_space=pltpu.VMEM),
        out_shape=jax.ShapeDtypeStruct((2 * rows, width), first.dtype),
        scratch_shapes=[pltpu.SemaphoreType.DMA((32,))],
        compiler_params=pltpu.CompilerParams(vmem_limit_bytes=8 << 20),
        cost_estimate=pl.CostEstimate(
            flops=0, bytes_accessed=8 * rows * width, transcendentals=0
        ),
    )(places, first, second)
    return out.reshape(4, rows // 2, width)


def total_over(vector, axes):
    spread = jnp.broadcast_to(vector[None], (16, vector.shape[0]))
    return jnp.sum(lax.all_to_all(spread, axes, 0, 0, tiled=True), axis=0)


def local(activations, out_grads, weights, momentum, scores, row_moment, col_moment):
    token_scale = 1.0 / math.sqrt(activations.shape[0] * 4)
    core, low = lax.axis_index("core"), lax.axis_index("zl")
    x, y = lax.axis_index("x"), lax.axis_index("y")
    rows = FF // 16

    def units(a, b):
        return lax.dynamic_slice_in_dim(out_grads, ((low ^ a) * 2 + (core ^ b)) * rows, rows, 1)

    low_blocks = swap(jnp.concatenate([units(1, 0), units(1, 1)], axis=0), "zl")
    near = units(0, 0)
    tokens = near.shape[0]
    near = jnp.concatenate([near, swap(units(0, 1), "core")], axis=0)
    away = jnp.concatenate([low_blocks[:tokens], swap(low_blocks[tokens:], "core")], axis=0)
    acts_core = swap(activations, "core")

    places = []
    for j in STEPS:
        for i in STEPS:
            dx, dy = jnp.where(core == 0, i, j), jnp.where(core == 0, j, i)
            places.append((x + dx) % 4 * 4 + (y + dy) % 4)
    places = jnp.stack(places).astype(jnp.int32)

    near = [*ring_start(near, 0), shift(near, 0, 2)]
    near[3:] = after(near[3:], away)
    (sent,) = after((activations,), *near)
    near = ring_start(jnp.concatenate(near, axis=0), 1)
    away = ring_end(ring_start(away, 0), 0, 1)
    half = sent.shape[0] // 2
    acts_low = (along_z(sent[:half], 1), along_z(sent[half:], -1))
    first = arranged(places, activations, acts_core)
    gradient = product(near[0], first[0]) + product(near[1], first[1]) + product(near[2], first[2])
    near = ring_end(after(near, *away), 1, 1)
    away = ring_start(jnp.concatenate(away, axis=0), 1)
    away[2], gradient = lax.optimization_barrier((away[2], gradient))
    away = ring_end(away, 1, -1)
    acts_low = jnp.concatenate(after(acts_low, away[2]), axis=0)
    second = arranged(places, acts_low, swap(acts_low, "core"))
    gradient = gradient + product(near[3], first[3])
    gradient = gradient + product(away[0], second[0]) + product(away[2], second[2])
    away[3], gradient = lax.optimization_barrier((away[3], gradient))
    gradient = gradient + product(away[3], second[3])
    away[1], gradient = lax.optimization_barrier((away[1], gradient))
    gradient = gradient + lax.optimization_barrier(product(away[1], second[1]))
    gradient = gradient * token_scale

    squares = gradient * gradient + 1e-30
    row_part, col_part = jnp.sum(squares, axis=1), jnp.sum(squares, axis=0)
    row_part, gradient = lax.optimization_barrier((row_part, gradient))
    scores_new = scores - 50.0 * weights * gradient
    row_full = total_over(row_part, ("x", "y"))
    row_moment_new = 0.8 * row_moment + 0.2 * row_full / D
    sums = jnp.concatenate([col_part, jnp.sum(row_moment_new.reshape(8, 128), axis=0)])
    sums = total_over(sums, ("zl", "core", "zh"))
    sums, scores_new, weights, gradient = lax.optimization_barrier(
        (sums, scores_new, weights, gradient)
    )
    col_moment_new = 0.8 * col_moment + 0.2 * sums[:512] / FF
    row_average = jnp.sum(sums[512:]) / FF
    row_scale, col_scale = lax.rsqrt(row_moment_new), lax.rsqrt(col_moment_new / row_average)
    update = gradient * (row_scale[:, None] * col_scale[None, :])
    momentum_new = (0.9 * momentum.astype(jnp.float32) + 0.1 * update).astype(jnp.bfloat16)
    weights_new = weights - 0.01 * momentum_new.astype(jnp.float32)
    return (weights_new, momentum_new, scores_new, row_moment_new, col_moment_new)


def solution(mesh):
    fine = Mesh(mesh.devices.reshape(2, 2, 4, 4, 4), ("zl", "core", "x", "y", "zh"))
    dp, row, col = ("zl", "core"), ("x", "y"), "zh"
    return jax.shard_map(
        local,
        mesh=fine,
        in_specs=(
            P(dp, row),
            P(dp + row, col),
            P((col,) + dp, row),
            P((col,) + dp, row),
            P((col,) + dp, row),
            P((col,) + dp),
            P(row),
        ),
        out_specs=(
            P((col,) + dp, row),
            P((col,) + dp, row),
            P((col,) + dp, row),
            P((col,) + dp),
            P(row),
        ),
        check_vma=False,
    )
```

```python
import math

import jax
import jax.numpy as jnp
from jax import lax
from jax.experimental import pallas as pl
from jax.experimental.pallas import tpu as pltpu
from jax.sharding import Mesh, PartitionSpec as P

D = 8192
FF = 16384
AXES = ("core", "x", "y")
STEPS = (0, -1, 1, 2)


def ring_pairs(phase, step):
    pairs = []
    for core in range(2):
        for x in range(4):
            for y in range(4):
                if core == phase:
                    to = (x + step) % 4 * 4 + y
                else:
                    to = x * 4 + (y + step) % 4
                pairs.append((core * 16 + x * 4 + y, core * 16 + to))
    return pairs


def shift(array, phase, step):
    return lax.ppermute(array, AXES, ring_pairs(phase, step))


def along_z(array, step):
    place = lambda z: z % 2 * 4 + z // 2
    return lax.ppermute(array, ("zl", "zh"), [(place(z), place((z + step) % 8)) for z in range(8)])


def swap(array, axis):
    return lax.ppermute(array, axis, [(0, 1), (1, 0)])


def ring_start(block, phase):
    return [block, shift(block, phase, 1), shift(block, phase, -1)]


def ring_end(blocks, phase, step):
    return [*blocks, shift(blocks[1] if step == 1 else blocks[2], phase, step)]


def after(blocks, *others):
    return lax.optimization_barrier((*blocks, *others))[: len(blocks)]


def product(grad_rows, act_rows):
    return lax.dot_general(
        grad_rows, act_rows, (((0,), (0,)), ((), ())), preferred_element_type=jnp.float32
    )


def arrange_kernel(place, first, second, out, sems):
    tokens = first.shape[0] // 16
    copies = []
    for i in range(16):
        rows = pl.ds(pl.multiple_of(place[i] * tokens, tokens), tokens)
        for c, source in enumerate((first, second)):
            at = pl.ds((2 * i + c) * tokens, tokens)
            copies.append(pltpu.make_async_copy(source.at[rows], out.at[at], sems.at[2 * i + c]))
    for copy in copies:
        copy.start()
    for copy in copies:
        copy.wait()


def arranged(places, first, second):
    rows, width = first.shape
    anywhere = pl.BlockSpec(memory_space=pl.ANY)
    out = pl.pallas_call(
        arrange_kernel,
        in_specs=[pl.BlockSpec(memory_space=pltpu.SMEM), anywhere, anywhere],
        out_specs=pl.BlockSpec(memory_space=pltpu.VMEM),
        out_shape=jax.ShapeDtypeStruct((2 * rows, width), first.dtype),
        scratch_shapes=[pltpu.SemaphoreType.DMA((32,))],
        compiler_params=pltpu.CompilerParams(vmem_limit_bytes=8 << 20),
        cost_estimate=pl.CostEstimate(
            flops=0, bytes_accessed=8 * rows * width, transcendentals=0
        ),
    )(places, first, second)
    return out.reshape(4, rows // 2, width)


def total_over(vector, axes):
    spread = jnp.broadcast_to(vector[None], (16, vector.shape[0]))
    return jnp.sum(lax.all_to_all(spread, axes, 0, 0, tiled=True), axis=0)


def local(activations, out_grads, weights, momentum, scores, row_moment, col_moment):
    token_scale = 1.0 / math.sqrt(activations.shape[0] * 4)
    core, low = lax.axis_index("core"), lax.axis_index("zl")
    x, y = lax.axis_index("x"), lax.axis_index("y")
    rows = FF // 16

    def units(a, b):
        return lax.dynamic_slice_in_dim(out_grads, ((low ^ a) * 2 + (core ^ b)) * rows, rows, 1)

    low_blocks = swap(jnp.concatenate([units(1, 0), units(1, 1)], axis=0), "zl")
    near = units(0, 0)
    tokens = near.shape[0]
    near = jnp.concatenate([near, swap(units(0, 1), "core")], axis=0)
    away = jnp.concatenate([low_blocks[:tokens], swap(low_blocks[tokens:], "core")], axis=0)
    acts_core = swap(activations, "core")

    places = []
    for j in STEPS:
        for i in STEPS:
            dx, dy = jnp.where(core == 0, i, j), jnp.where(core == 0, j, i)
            places.append((x + dx) % 4 * 4 + (y + dy) % 4)
    places = jnp.stack(places).astype(jnp.int32)

    near = [*ring_start(near, 0), shift(near, 0, 2)]
    near[3:] = after(near[3:], away)
    (sent,) = after((activations,), *near)
    near = ring_start(jnp.concatenate(near, axis=0), 1)
    away = ring_end(ring_start(away, 0), 0, 1)
    first = arranged(places, activations, acts_core)
    away[2], first = lax.optimization_barrier((away[2], first))
    half = sent.shape[0] // 2
    acts_low = (along_z(sent[:half], 1), along_z(sent[half:], -1))
    gradient = product(near[0], first[0]) + product(near[1], first[1]) + product(near[2], first[2])
    near = ring_end(after(near, *away), 1, 1)
    away = ring_start(jnp.concatenate(away, axis=0), 1)
    away[2], gradient = lax.optimization_barrier((away[2], gradient))
    away = ring_end(away, 1, -1)
    acts_low = jnp.concatenate(after(acts_low, away[2]), axis=0)
    second = arranged(places, acts_low, swap(acts_low, "core"))
    gradient = gradient + product(near[3], first[3])
    gradient = gradient + product(away[0], second[0]) + product(away[2], second[2])
    away[3], gradient = lax.optimization_barrier((away[3], gradient))
    gradient = gradient + product(away[3], second[3])
    away[1], gradient = lax.optimization_barrier((away[1], gradient))
    gradient = gradient + lax.optimization_barrier(product(away[1], second[1]))
    gradient = gradient * token_scale

    squares = gradient * gradient + 1e-30
    row_part, col_part = jnp.sum(squares, axis=1), jnp.sum(squares, axis=0)
    row_part, gradient = lax.optimization_barrier((row_part, gradient))
    scores_new = scores - 50.0 * weights * gradient
    row_full = total_over(row_part, ("x", "y"))
    row_moment_new = 0.8 * row_moment + 0.2 * row_full / D
    sums = jnp.concatenate([col_part, jnp.sum(row_moment_new.reshape(8, 128), axis=0)])
    sums = total_over(sums, ("zl", "core", "zh"))
    sums, scores_new, weights, gradient = lax.optimization_barrier(
        (sums, scores_new, weights, gradient)
    )
    col_moment_new = 0.8 * col_moment + 0.2 * sums[:512] / FF
    row_average = jnp.sum(sums[512:]) / FF
    row_scale, col_scale = lax.rsqrt(row_moment_new), lax.rsqrt(col_moment_new / row_average)
    update = gradient * (row_scale[:, None] * col_scale[None, :])
    momentum_new = (0.9 * momentum.astype(jnp.float32) + 0.1 * update).astype(jnp.bfloat16)
    weights_new = weights - 0.01 * momentum_new.astype(jnp.float32)
    return (weights_new, momentum_new, scores_new, row_moment_new, col_moment_new)


def solution(mesh):
    fine = Mesh(mesh.devices.reshape(2, 2, 4, 4, 4), ("zl", "core", "x", "y", "zh"))
    dp, row, col = ("zl", "core"), ("x", "y"), "zh"
    return jax.shard_map(
        local,
        mesh=fine,
        in_specs=(
            P(dp, row),
            P(dp + row, col),
            P((col,) + dp, row),
            P((col,) + dp, row),
            P((col,) + dp, row),
            P((col,) + dp),
            P(row),
        ),
        out_specs=(
            P((col,) + dp, row),
            P((col,) + dp, row),
            P((col,) + dp, row),
            P((col,) + dp),
            P(row),
        ),
        check_vma=False,
    )
```
